32 devices in a mesh: tile: 8 (over z, x), depth: 4 (over y, core).
Axes of the slice: x: 2, y: 2, z: 4, core: 2. Of those that a mesh axis runs over, the one named last changes fastest.
Arguments:
- phase: float32 [64, 512, 256], P('tile', 'depth'), may hold values from -1 to 1
- solute: float32 [64, 512, 256], P('tile', 'depth'), may hold values from -3 to 3
- dphase: float32 [64, 512, 256], P('tile', 'depth'), may hold values from -6 to 6
- dsolute: float32 [64, 512, 256], P('tile', 'depth'), may hold values from -6 to 6
- labels: int32 [64, 256], P('tile'), may hold values from 0 to 3
- pixel_mask: int32 [64, 256], P('tile'), may hold values 0 or 1
Outputs:
- hess_phase: float32 [64, 512, 256], P('tile', 'depth')
- hess_solute: float32 [64, 512, 256], P('tile', 'depth')
- change: float32 [64, 256], P('tile')
The draws below stay inside these ranges and needn't reach their ends.
All inputs are finite; a program needn't handle non-finite values. No bound on the sum of `pixel_mask` on one device may be relied on, other than what follows from the above.
Results may differ from the reference program's by a relative error of at most 0.00002.
Values sent between devices are 32-bit elements; how exact they have to be, the bound alone decides.
A program may use at most 64 MiB of HBM per device.

```python
import jax
import jax.numpy as jnp
from jax import lax

NY = 256
NX = 64
NZ = 512


def set_ends(result, key, smallest, largest):
    dims = result.shape
    index_at = [jax.random.randint(jax.random.fold_in(key, axis), (), 0, dims[axis]) for axis in range(len(dims))]
    result = result.at[tuple(index_at)].set(smallest)
    longest = dims.index(max(dims))
    index_at[longest] = (index_at[longest] + 1) % dims[longest]
    return result.at[tuple(index_at)].set(largest)


def levels(own_key, shape, split, low, high):
    def one(position, shards_of):
        heights = jax.random.uniform(jax.random.fold_in(jax.random.fold_in(own_key, 6), position), (shards_of,), jnp.float32, low / len(split), high / len(split))
        return jnp.repeat(jnp.exp(heights), shape[position] // shards_of).reshape((-1,) + (1,) * (len(shape) - position - 1))

    loudness = one(*split[0])
    for cut in split[1:]:
        loudness = loudness * one(*cut)
    return loudness


def normal_values(stream_key, dims, spread, most, shards=(), dtype=jnp.bfloat16):
    drawn = jax.random.normal(stream_key, dims, jnp.float32) * spread
    if len(shards) > 0:
        drawn = levels(stream_key, dims, shards, -0.22, 0.18) * drawn
    return jnp.clip(drawn, min=-most, max=most).astype(dtype)


def setup_inputs(seed: int = 0) -> dict:
    arg_keys = jax.random.split(jax.random.key(seed), 7)
    phase = jnp.clip(jax.random.uniform(arg_keys[0], (NX, NZ, NY), jnp.float32, -1.0, 1.0) * levels(arg_keys[0], (NX, NZ, NY), ((0, 8), (1, 4)), -0.4, 0.0), -1.0, 1.0)
    solute = normal_values(arg_keys[1], (NX, NZ, NY), 0.5, 3.0, ((0, 8), (1, 4)), jnp.float32)
    dphase = normal_values(arg_keys[2], (NX, NZ, NY), 1.0, 6.0, ((0, 8), (1, 4)), jnp.float32)
    dsolute = normal_values(arg_keys[3], (NX, NZ, NY), 1.0, 6.0, ((0, 8), (1, 4)), jnp.float32)
    labels = set_ends(jax.random.randint(arg_keys[4], (NX, NY), 0, 4), jax.random.fold_in(arg_keys[4], 1), 0, 3).astype(jnp.int32)
    pixel_mask = set_ends((jax.random.randint(arg_keys[5], (NX, NY), 0, 4) < 3).astype(jnp.int32), jax.random.fold_in(arg_keys[5], 1), 0, 1)
    return dict(phase=phase, solute=solute, dphase=dphase, dsolute=dsolute, labels=labels, pixel_mask=pixel_mask)


step_size = 0.1
rejection = 0.5

def laplace(field):
    padded = jnp.pad(field, 1)
    total = padded[2:, 1:-1, 1:-1] + padded[:-2, 1:-1, 1:-1]
    total = total + padded[1:-1, 2:, 1:-1] + padded[1:-1, :-2, 1:-1]
    total = total + padded[1:-1, 1:-1, 2:] + padded[1:-1, 1:-1, :-2]
    return total - 6.0 * field

def growth(labels):
    return jnp.where(labels == 0, 0.6, jnp.where(labels == 1, 1.0, jnp.where(labels == 2, 1.7, 0.8))).astype(jnp.float32)

def slopes(phase, solute, grow):
    shell = 1.0 - phase * phase
    return (grow * (1.0 - 3.0 * phase * phase) + 4.0 * phase * shell * solute, -shell * shell)

def reference(phase, solute, dphase, dsolute, labels, pixel_mask):
    grow = growth(labels)[:, None, :]
    saved = []
    for section in range(2):
        slope_phase, slope_solute = slopes(phase, solute, grow)
        saved.append((slope_phase, slope_solute))
        shell = 1.0 - phase * phase
        phase_next = phase + step_size * (laplace(phase) + grow * (phase - phase * phase * phase) - shell * shell * solute)
        solute_next = solute + step_size * laplace(solute) + rejection * (phase_next - phase)
        dphase_next = dphase + step_size * (laplace(dphase) + slope_phase * dphase + slope_solute * dsolute)
        dsolute_next = dsolute + step_size * laplace(dsolute) + rejection * (dphase_next - dphase)
        phase, solute, dphase, dsolute = (phase_next, solute_next, dphase_next, dsolute_next)
    depth_root = jnp.sqrt(jnp.float32(NZ))
    bright = jnp.exp(-lax.optimization_barrier(jnp.sum(solute, axis=1)) / depth_root)
    change = -bright * lax.optimization_barrier(jnp.sum(dsolute, axis=1)) / depth_root
    backdrop = -bright * pixel_mask.astype(jnp.float32) * change
    adj_solute = jnp.broadcast_to(backdrop[:, None, :], phase.shape)
    adj_phase = jnp.zeros_like(phase)
    for section in (1, 0):
        slope_phase, slope_solute = saved[section]
        carried = adj_phase + rejection * adj_solute
        adj_phase = carried + step_size * (laplace(carried) + slope_phase * carried) - rejection * adj_solute
        adj_solute = adj_solute + step_size * laplace(adj_solute) + step_size * slope_solute * carried
    return (adj_phase, adj_solute, change)
```

```python
import functools
import math

import jax
import jax.numpy as jnp
from jax import lax
from jax.experimental import pallas as pl
from jax.experimental.pallas import tpu as pltpu
from jax.sharding import PartitionSpec as P

MESH = pl.DeviceIdType.MESH
PAD = 16
CH = 24
BC = 32


def growth(labels):
    return jnp.where(
        labels == 0, 0.6, jnp.where(labels == 1, 1.0, jnp.where(labels == 2, 1.7, 0.8))
    ).astype(jnp.float32)


def slopes(p, s, grow):
    shell = 1.0 - p * p
    return grow * (1.0 - 3.0 * p * p) + 4.0 * p * shell * s, -shell * shell


def tiles(block, count):
    return jnp.concatenate([block] * count, axis=0)


def fold(value):
    total = value[0:8]
    for k in range(8, value.shape[0], 8):
        total = total + value[k : k + 8]
    return total


def lanes(value):
    cols = value.shape[1]
    lane = lax.broadcasted_iota(jnp.int32, value.shape, 1)
    left = jnp.where(lane == 0, 0.0, pltpu.roll(value, 1, 1))
    right = jnp.where(lane == cols - 1, 0.0, pltpu.roll(value, cols - 1, 1))
    return left + right


def kernel(
    nt, nd,
    p_hbm, s_hbm, dp_hbm, ds_hbm, lab_hbm, mask_hbm,
    hp_hbm, hs_hbm, change_ref,
    pe, se, dpe, dse, labe, maske, growb,
    c1, a1, wide, solw, hp, hs,
    accs, cross, own_out, up_out, down_out, own_in, up_in, down_in,
    ext, bb, gb, hb,
    local_sem, out_sem, send_sem, recv_sem, own_send, own_recv, up_send, up_recv, down_send, down_recv,
):
    rows, depth, cols = p_hbm.shape
    t = lax.axis_index("tile")
    d = lax.axis_index("depth")
    has_above, has_below = t < nt - 1, t > 0
    has_right, has_left = d < nd - 1, d > 0
    above, below = lax.rem(t + 1, nt), lax.rem(t + nt - 1, nt)
    right, left = lax.rem(d + 1, nd), lax.rem(d + nd - 1, nd)
    end = PAD + depth
    core = slice(PAD, end)
    core_rows = slice(2, 2 + rows)

    local = [
        pltpu.make_async_copy(src, dst, local_sem.at[n])
        for n, (src, dst) in enumerate(
            [
                (p_hbm, pe.at[core_rows, core]),
                (s_hbm, se.at[core_rows, core]),
                (dp_hbm, dpe.at[:, core]),
                (ds_hbm, dse.at[:, core]),
                (lab_hbm, labe.at[rows : 2 * rows]),
                (mask_hbm, maske.at[rows : 2 * rows]),
            ]
        )
    ]
    for copy in local:
        copy.start()

    barrier = pltpu.get_barrier_semaphore()

    def greet(tt, dd):
        pl.semaphore_signal(barrier, inc=1, device_id=(tt, dd), device_id_type=MESH)

    for n in range(1, nd):
        greet(t, lax.rem(d + n, nd))

    @pl.when(has_above)
    def _():
        for n in range(nd):
            greet(above, n)

    @pl.when(has_below)
    def _():
        for n in range(nd):
            greet(below, n)

    beside_count = jnp.where(has_above, 1, 0) + jnp.where(has_below, 1, 0)
    pl.semaphore_wait(barrier, nd - 1 + nd * beside_count)

    number = [0]

    def remote(src, dst, tt, dd):
        n = number[0]
        number[0] = n + 1
        return pltpu.make_async_remote_copy(
            src_ref=src,
            dst_ref=dst,
            send_sem=send_sem.at[n],
            recv_sem=recv_sem.at[n],
            device_id=(tt, dd),
            device_id_type=MESH,
        )

    top, bottom = 2 + rows, 1
    first, last = slice(0, 8), slice(depth - 8, depth)
    after, before = slice(end, end + 8), slice(PAD - 8, PAD)
    pairs = [(p_hbm, pe), (s_hbm, se)]
    to_right = [remote(a.at[:, last], b.at[core_rows, before], t, right) for a, b in pairs]
    to_left = [remote(a.at[:, first], b.at[core_rows, after], t, left) for a, b in pairs]
    for a, b in [(dp_hbm, dpe), (ds_hbm, dse)]:
        to_right.append(remote(a.at[:, last], b.at[:, before], t, right))
        to_left.append(remote(a.at[:, first], b.at[:, after], t, left))
    diagonals = []
    for tt, going_t, coming_t, src_row, dst_row in [
        (above, has_above, has_below, rows - 1, bottom),
        (below, has_below, has_above, 0, top),
    ]:
        for dd, going_d, coming_d, src_k, dst_k in [
            (right, has_right, has_left, last, before),
            (left, has_left, has_right, first, after),
        ]:
            copies = [
                remote(a.at[pl.ds(src_row, 1), src_k], b.at[pl.ds(dst_row, 1), dst_k], tt, dd)
                for a, b in pairs
            ]
            diagonals.append((going_t & going_d, coming_t & coming_d, copies, dst_row, dst_k))
    up_near = [remote(lab_hbm, labe.at[0:rows], above, d), remote(mask_hbm, maske.at[0:rows], above, d)]
    down_near = [
        remote(lab_hbm, labe.at[2 * rows : 3 * rows], below, d),
        remote(mask_hbm, maske.at[2 * rows : 3 * rows], below, d),
    ]
    for a, b in pairs:
        up_near.append(remote(a.at[pl.ds(rows - 1, 1)], b.at[pl.ds(1, 1), core], above, d))
        down_near.append(remote(a.at[pl.ds(0, 1)], b.at[pl.ds(top, 1), core], below, d))
    up_far = [remote(a.at[pl.ds(rows - 2, 1)], b.at[pl.ds(0, 1), core], above, d) for a, b in pairs]
    down_far = [remote(a.at[pl.ds(1, 1)], b.at[pl.ds(top + 1, 1), core], below, d) for a, b in pairs]

    def start(condition, copies):
        @pl.when(condition)
        def _():
            for copy in copies:
                copy.start()

    def arrive(condition, copies):
        @pl.when(condition)
        def _():
            for copy in copies:
                copy.wait_recv()

    def sent(condition, copies):
        @pl.when(condition)
        def _():
            for copy in copies:
                copy.wait_send()

    start(has_above, up_near)
    start(has_below, down_near)
    start(has_right, to_right)
    start(has_left, to_left)
    for going, coming, copies, _, _ in diagonals:
        start(going, copies)
    start(has_above, up_far)
    start(has_below, down_far)

    row_zero = jnp.zeros((depth, cols), jnp.float32)
    tile_zero = jnp.zeros((8, cols), jnp.float32)
    label_zero = jnp.zeros((rows, cols), jnp.int32)

    def no_row(condition, near, far, label_at):
        @pl.when(jnp.logical_not(condition))
        def _():
            for b in (pe, se):
                b[near, core] = row_zero
                b[far, core] = row_zero
            labe[label_at : label_at + rows] = label_zero
            maske[label_at : label_at + rows] = label_zero

    no_row(has_below, 1, 0, 0)
    no_row(has_above, top, top + 1, 2 * rows)

    def no_side(condition, span):
        @pl.when(jnp.logical_not(condition))
        def _():
            for r in range(rows):
                pe[2 + r, span] = tile_zero
                se[2 + r, span] = tile_zero
                dpe[r, span] = tile_zero
                dse[r, span] = tile_zero

    no_side(has_left, before)
    no_side(has_right, after)
    for _, coming, _, dst_row, dst_k in diagonals:

        @pl.when(jnp.logical_not(coming))
        def _():
            pe[dst_row, dst_k] = tile_zero
            se[dst_row, dst_k] = tile_zero

    for copy in local:
        copy.wait()

    def set_growth(j):
        row = labe[rows - 1 + j : rows + j]
        growb[j] = jnp.broadcast_to(growth(row), (8, cols))

    for j in range(1, rows + 1):
        set_growth(j)

    sub = lax.broadcasted_iota(jnp.int32, (CH, cols), 0)
    low_end = jnp.where(d == 0, PAD, -1)
    high_end = jnp.where(d == nd - 1, end - 1, -1)

    def spread(ref, r, k0):
        block = ref[r, pl.ds(pl.multiple_of(k0 - 8, 8), CH + 16), :]
        size = CH + 16
        beside = pltpu.roll(block, 1, 0) + pltpu.roll(block, size - 1, 0)
        center = block[8 : 8 + CH]
        return center, beside[8 : 8 + CH] + lanes(center) - 6.0 * center

    def at(ref, r, k0):
        return ref[r, pl.ds(pl.multiple_of(k0, 8), CH), :]

    def base_next(i, k0, grow):
        p, lap_p = spread(pe, i, k0)
        s, lap_s = spread(se, i, k0)
        lap_p = lap_p + at(pe, i - 1, k0) + at(pe, i + 1, k0)
        lap_s = lap_s + at(se, i - 1, k0) + at(se, i + 1, k0)
        shell = 1.0 - p * p
        p_next = p + 0.1 * (lap_p + grow * (p - p * p * p) - shell * shell * s)
        s_next = s + 0.1 * lap_s + 0.5 * (p_next - p)
        return p, s, p_next, s_next

    def save_slopes(i, k0, slope_p, slope_s, at_end):
        span = pl.ds(pl.multiple_of(k0, 8), CH)
        c1[i - 1, span, :] = 0.05 * slope_p + 0.025 * slope_s - 0.1 * at_end
        a1[i - 1, span, :] = 0.05 * slope_s - 0.1 * at_end

    def ends_of(k0):
        k = sub + k0
        at_end = jnp.where((k == low_end) | (k == high_end), 1.0, 0.0)
        inside = (k >= PAD) & (k < end)
        return at_end, inside

    chunks = (depth + 16) // CH

    def own_row(i, has_lower, has_upper):
        j = i - 2
        grow = tiles(growb[i - 1], CH // 8)

        def one(n, carry):
            k0 = PAD - 8 + n * CH
            at_end, inside = ends_of(k0)
            p, s, p1, s1 = base_next(i, k0, grow)
            slope_p, slope_s = slopes(p, s, grow)
            span = pl.ds(pl.multiple_of(k0, 8), CH)
            wide[j, span, :] = 0.4 + 0.1 * slope_p
            solw[j, span, :] = 0.1 * slope_s
            next_p, next_s = slopes(p1, s1, grow)
            save_slopes(i, k0, next_p, next_s, at_end)
            dp, lap_dp = spread(dpe, j, k0)
            ds, lap_ds = spread(dse, j, k0)
            if has_lower:
                lap_dp = lap_dp + at(dpe, j - 1, k0)
                lap_ds = lap_ds + at(dse, j - 1, k0)
            if has_upper:
                lap_dp = lap_dp + at(dpe, j + 1, k0)
                lap_ds = lap_ds + at(dse, j + 1, k0)
            dp1 = dp + 0.1 * (lap_dp + slope_p * dp + slope_s * ds)
            ds1 = ds + 0.1 * lap_ds + 0.5 * (dp1 - dp)
            weight = 4.0 + at_end
            blend = 0.1 * s1 + 0.05 * p1
            dblend = 0.1 * ds1 + 0.05 * dp1
            term = s1 + 0.05 * (grow * (p1 - p1 * p1 * p1) + next_s * s1) - weight * blend
            dterm = ds1 + 0.05 * (next_p * dp1 + next_s * ds1) - weight * dblend
            parts = (term, blend, dterm, dblend)
            return tuple(c + fold(jnp.where(inside, v, 0.0)) for c, v in zip(carry, parts))

        zero = jnp.zeros((8, cols), jnp.float32)
        sums = lax.fori_loop(0, chunks, one, (zero, zero, zero, zero))
        for q in range(4):
            accs[q, j] = sums[q]

    def halo_row(i, j, slot):
        grow = tiles(growb[i - 1], CH // 8)

        def one(n, carry):
            k0 = PAD - 8 + n * CH
            at_end, inside = ends_of(k0)
            _, _, p1, s1 = base_next(i, k0, grow)
            next_p, next_s = slopes(p1, s1, grow)
            save_slopes(i, k0, next_p, next_s, at_end)
            dp, ds = at(dpe, j, k0), at(dse, j, k0)
            add_p = 0.1 * dp
            add_s = 0.1 * ds + 0.05 * dp
            dblend = 0.1 * add_s + 0.05 * add_p
            dterm = add_s + 0.05 * (next_p * add_p + next_s * add_s) - (4.0 + at_end) * dblend
            return tuple(
                c + fold(jnp.where(inside, v, 0.0)) for c, v in zip(carry, (dterm, dblend))
            )

        zero = jnp.zeros((8, cols), jnp.float32)
        sums = lax.fori_loop(0, chunks, one, (zero, zero))
        cross[slot] = sums[0]
        cross[slot + 1] = sums[1]

    def no_halo_row(i, slot):
        c1[i - 1] = jnp.zeros((end + PAD, cols), jnp.float32)
        a1[i - 1] = jnp.zeros((end + PAD, cols), jnp.float32)
        cross[slot] = tile_zero
        cross[slot + 1] = tile_zero

    arrive(has_left, to_right)
    arrive(has_right, to_left)

    def middle(i, carry):
        own_row(i, True, True)
        return carry

    lax.fori_loop(3, rows + 1, middle, 0)
    for _, coming, copies, _, _ in diagonals:
        arrive(coming, copies)
    arrive(has_below, up_near)
    arrive(has_above, down_near)
    set_growth(0)
    set_growth(rows + 1)
    own_row(2, False, True)
    own_row(rows + 1, True, False)

    arrive(has_below, up_far)
    arrive(has_above, down_far)

    @pl.when(has_below)
    def _():
        halo_row(1, 0, 0)

    @pl.when(jnp.logical_not(has_below))
    def _():
        no_halo_row(1, 0)

    @pl.when(has_above)
    def _():
        halo_row(rows + 2, rows - 1, 2)

    @pl.when(jnp.logical_not(has_above))
    def _():
        no_halo_row(rows + 2, 2)

    place = lax.broadcasted_iota(jnp.int32, (rows, cols), 0)

    def beside_rows(x):
        return jnp.where(place == 0, 0.0, pltpu.roll(x, 1, 0)) + jnp.where(
            place == rows - 1, 0.0, pltpu.roll(x, rows - 1, 0)
        )

    term, blend, dterm, dblend = [jnp.sum(accs[q], axis=1) for q in range(4)]
    x_low, q_low, x_high, q_high = [jnp.sum(cross[q], axis=0, keepdims=True) for q in range(4)]
    own_s = term + lanes(blend) + beside_rows(blend)
    own_d = dterm + lanes(dblend) + beside_rows(dblend)
    own_d = own_d + jnp.where(place == 0, q_low, 0.0) + jnp.where(place == rows - 1, q_high, 0.0)
    low_d = dblend[0:1] + x_low + lanes(q_low)
    high_d = dblend[rows - 1 : rows] + x_high + lanes(q_high)
    line = jnp.zeros((1, cols), jnp.float32)
    own_out[0:rows] = own_s
    own_out[rows : 2 * rows] = own_d
    tail = 2 * rows
    halo = [line, blend[0:1], blend[rows - 1 : rows], line, q_low, low_d, high_d, q_high]
    for n, value in enumerate(halo):
        own_out[tail + n : tail + n + 1] = value
    up_out[0:2] = own_s[rows - 2 : rows]
    up_out[2:3] = halo[2]
    up_out[3:4] = line
    up_out[4:6] = own_d[rows - 2 : rows]
    up_out[6:7] = high_d
    up_out[7:8] = q_high
    down_out[0:1] = line
    down_out[1:2] = halo[1]
    down_out[2:4] = own_s[0:2]
    down_out[4:5] = q_low
    down_out[5:6] = low_d
    down_out[6:8] = own_d[0:2]

    def message(src, inbox, sends, receives, n, slot, tt, dd):
        return pltpu.make_async_remote_copy(
            src_ref=src,
            dst_ref=inbox.at[slot],
            send_sem=sends.at[n],
            recv_sem=receives.at[slot],
            device_id=(tt, dd),
            device_id_type=MESH,
        )

    own_messages = [
        message(own_out, own_in, own_send, own_recv, n - 1, d, t, lax.rem(d + n, nd))
        for n in range(1, nd)
    ]
    up_messages = [message(up_out, up_in, up_send, up_recv, n, d, above, n) for n in range(nd)]
    down_messages = [
        message(down_out, down_in, down_send, down_recv, n, d, below, n) for n in range(nd)
    ]
    start(has_above, up_messages)
    start(has_below, down_messages)
    for copy in own_messages:
        copy.start()
    own_in[d] = own_out[...]

    @pl.when(jnp.logical_not(has_below))
    def _():
        for n in range(nd):
            up_in[n] = tile_zero

    @pl.when(jnp.logical_not(has_above))
    def _():
        for n in range(nd):
            down_in[n] = tile_zero

    ext[...] = jnp.zeros_like(ext)
    for n in range(1, nd):
        slot = lax.rem(d + n, nd)
        message(own_out, own_in, own_send, own_recv, n - 1, slot, t, slot).wait_recv()

    @pl.when(has_below)
    def _():
        for n in range(nd):
            message(up_out, up_in, up_send, up_recv, n, n, above, n).wait_recv()

    @pl.when(has_above)
    def _():
        for n in range(nd):
            message(down_out, down_in, down_send, down_recv, n, n, below, n).wait_recv()

    total, low, high = own_in[0], up_in[0], down_in[0]
    for n in range(1, nd):
        total, low, high = total + own_in[n], low + up_in[n], high + down_in[n]
    for q in range(2):
        ext[q, 0:2] = total[tail + 4 * q : tail + 4 * q + 2] + low[4 * q : 4 * q + 2]
        ext[q, 2 : 2 + rows] = total[q * rows : (q + 1) * rows]
        ext[q, 2:4] += low[4 * q + 2 : 4 * q + 4]
        ext[q, rows : rows + 2] += high[4 * q : 4 * q + 2]
        ext[q, rows + 2 : rows + 4] = (
            total[tail + 4 * q + 2 : tail + 4 * q + 4] + high[4 * q + 2 : 4 * q + 4]
        )
    root = math.sqrt(depth * nd)
    high_rows = ext.shape[1]
    bright = jnp.exp(-ext[0] / root)
    change = -bright * ext[1] / root
    mask = maske[rows - 2 : rows - 2 + high_rows].astype(jnp.float32)
    where = lax.broadcasted_iota(jnp.int32, (high_rows, cols), 0)
    valid = jnp.where(has_below, 0, 2)
    valid_end = jnp.where(has_above, rows + 4, rows + 2)
    inside_rows = (where >= valid) & (where < valid_end)
    back = jnp.where(inside_rows, -bright * mask * change, 0.0)
    change_ref[...] = change[2 : 2 + rows]
    flat = pltpu.roll(back, 1, 0) + pltpu.roll(back, high_rows - 1, 0) + lanes(back) - 4.0 * back
    flat = jnp.where(inside_rows, flat, 0.0)
    g = 0.5 * back + 0.1 * flat
    h = back + 0.1 * flat
    for j in range(rows + 2):
        bb[j] = jnp.broadcast_to(back[j + 1 : j + 2], (8, cols))
        gb[j] = jnp.broadcast_to(g[j + 1 : j + 2], (8, cols))
        hb[j] = jnp.broadcast_to(h[j + 1 : j + 2], (8, cols))

    def carry_row(j, carry):
        b, gg, hh = [tiles(x[j], CH // 8) for x in (bb, gb, hb)]
        for n in range(chunks):
            span = slice(PAD - 8 + n * CH, PAD - 8 + (n + 1) * CH)
            c1[j, span] = gg + c1[j, span] * b
            a1[j, span] = hh + a1[j, span] * b
        return carry

    lax.fori_loop(0, rows + 2, carry_row, 0)

    def no_depth(condition, span):
        @pl.when(jnp.logical_not(condition))
        def _():
            for j in range(rows + 2):
                c1[j, span] = tile_zero
                a1[j, span] = tile_zero

    no_depth(has_left, before)
    no_depth(has_right, after)

    def near(ref, j, k0):
        size = BC + 16
        block = ref[j, k0 - 8 : k0 - 8 + size]
        beside = pltpu.roll(block, 1, 0) + pltpu.roll(block, size - 1, 0)
        center = block[8 : 8 + BC]
        span = slice(k0, k0 + BC)
        return center, beside[8 : 8 + BC] + lanes(center) + ref[j - 1, span] + ref[j + 1, span]

    def out_copies(j):
        return [
            pltpu.make_async_copy(hp.at[j], hp_hbm.at[j], out_sem.at[0, j]),
            pltpu.make_async_copy(hs.at[j], hs_hbm.at[j], out_sem.at[1, j]),
        ]

    def finish(j, carry):
        for n in range(depth // BC):
            k0 = PAD + n * BC
            c, near_c = near(c1, j + 1, k0)
            a, near_a = near(a1, j + 1, k0)
            span = slice(k0, k0 + BC)
            dst = slice(n * BC, (n + 1) * BC)
            hp[j, dst] = c * wide[j, span] + 0.1 * near_c - 0.5 * a
            hs[j, dst] = 0.4 * a + 0.1 * near_a + solw[j, span] * c
        for copy in out_copies(j):
            copy.start()
        return carry

    lax.fori_loop(0, rows, finish, 0)
    for copy in own_messages:
        copy.wait_send()
    sent(has_above, up_messages + up_near + up_far)
    sent(has_below, down_messages + down_near + down_far)
    sent(has_right, to_right)
    sent(has_left, to_left)
    for going, coming, copies, _, _ in diagonals:
        sent(going, copies)
    for j in range(rows):
        for copy in out_copies(j):
            copy.wait()


def local(nt, nd, phase, solute, dphase, dsolute, labels, pixel_mask):
    rows, depth, cols = phase.shape
    f32, i32 = jnp.float32, jnp.int32
    length = depth + 2 * PAD
    dma = pltpu.SemaphoreType.DMA
    any_space = pl.BlockSpec(memory_space=pl.ANY)
    vmem = pl.BlockSpec(memory_space=pltpu.VMEM)
    field = jax.ShapeDtypeStruct((rows, depth, cols), f32)
    return pl.pallas_call(
        functools.partial(kernel, nt, nd),
        out_shape=(field, field, jax.ShapeDtypeStruct((rows, cols), f32)),
        in_specs=[any_space] * 6,
        out_specs=(any_space, any_space, vmem),
        scratch_shapes=[
            pltpu.VMEM((rows + 4, length, cols), f32),
            pltpu.VMEM((rows + 4, length, cols), f32),
            pltpu.VMEM((rows, length, cols), f32),
            pltpu.VMEM((rows, length, cols), f32),
            pltpu.VMEM((3 * rows, cols), i32),
            pltpu.VMEM((3 * rows, cols), i32),
            pltpu.VMEM((rows + 2, 8, cols), f32),
            pltpu.VMEM((rows + 2, length, cols), f32),
            pltpu.VMEM((rows + 2, length, cols), f32),
            pltpu.VMEM((rows, length, cols), f32),
            pltpu.VMEM((rows, length, cols), f32),
            pltpu.VMEM((rows, depth, cols), f32),
            pltpu.VMEM((rows, depth, cols), f32),
            pltpu.VMEM((4, rows, 8, cols), f32),
            pltpu.VMEM((4, 8, cols), f32),
            pltpu.VMEM((2 * rows + 8, cols), f32),
            pltpu.VMEM((8, cols), f32),
            pltpu.VMEM((8, cols), f32),
            pltpu.VMEM((nd, 2 * rows + 8, cols), f32),
            pltpu.VMEM((nd, 8, cols), f32),
            pltpu.VMEM((nd, 8, cols), f32),
            pltpu.VMEM((2, rows + 8, cols), f32),
            pltpu.VMEM((rows + 2, 8, cols), f32),
            pltpu.VMEM((rows + 2, 8, cols), f32),
            pltpu.VMEM((rows + 2, 8, cols), f32),
            dma((6,)),
            dma((2, rows)),
            dma((28,)),
            dma((28,)),
            dma((nd - 1,)),
            dma((nd,)),
            dma((nd,)),
            dma((nd,)),
            dma((nd,)),
            dma((nd,)),
        ],
        compiler_params=pltpu.CompilerParams(
            collective_id=0, has_side_effects=True, vmem_limit_bytes=48 * 1024 * 1024
        ),
    )(phase, solute, dphase, dsolute, labels, pixel_mask)


def solution(mesh):
    field, plane = P("tile", "depth", None), P("tile", None)
    return jax.shard_map(
        functools.partial(local, mesh.shape["tile"], mesh.shape["depth"]),
        mesh=mesh,
        in_specs=(field, field, field, field, plane, plane),
        out_specs=(field, field, plane),
        check_vma=False,
    )
```

```python
import functools
import math

import jax
import jax.numpy as jnp
from jax import lax
from jax.experimental import pallas as pl
from jax.experimental.pallas import tpu as pltpu
from jax.sharding import PartitionSpec as P

MESH = pl.DeviceIdType.MESH
PAD = 16
CH = 24
BC = 32


def growth(labels):
    return jnp.where(
        labels == 0, 0.6, jnp.where(labels == 1, 1.0, jnp.where(labels == 2, 1.7, 0.8))
    ).astype(jnp.float32)


def slopes(p, s, grow):
    shell = 1.0 - p * p
    return grow * (1.0 - 3.0 * p * p) + 4.0 * p * shell * s, -shell * shell


def tiles(block, count):
    return jnp.concatenate([block] * count, axis=0)


def fold(value):
    total = value[0:8]
    for k in range(8, value.shape[0], 8):
        total = total + value[k : k + 8]
    return total


def lanes(value):
    cols = value.shape[1]
    lane = lax.broadcasted_iota(jnp.int32, value.shape, 1)
    left = jnp.where(lane == 0, 0.0, pltpu.roll(value, 1, 1))
    right = jnp.where(lane == cols - 1, 0.0, pltpu.roll(value, cols - 1, 1))
    return left + right


def kernel(
    nt, nd,
    p_hbm, s_hbm, dp_hbm, ds_hbm, lab_hbm, mask_hbm,
    hp_hbm, hs_hbm, change_ref,
    pe, se, dpe, dse, labe, maske, growb,
    c1, a1, wide, solw, hp, hs,
    accs, cross, own_out, up_out, down_out, own_in, up_in, down_in,
    ext, bb, gb, hb,
    local_sem, out_sem, send_sem, recv_sem, own_send, own_recv, up_send, up_recv, down_send, down_recv,
):
    rows, depth, cols = p_hbm.shape
    t = lax.axis_index("tile")
    d = lax.axis_index("depth")
    has_above, has_below = t < nt - 1, t > 0
    has_right, has_left = d < nd - 1, d > 0
    above, below = lax.rem(t + 1, nt), lax.rem(t + nt - 1, nt)
    right, left = lax.rem(d + 1, nd), lax.rem(d + nd - 1, nd)
    end = PAD + depth
    core = slice(PAD, end)
    core_rows = slice(2, 2 + rows)

    local = [
        pltpu.make_async_copy(src, dst, local_sem.at[n])
        for n, (src, dst) in enumerate(
            [
                (p_hbm, pe.at[core_rows, core]),
                (s_hbm, se.at[core_rows, core]),
                (dp_hbm, dpe.at[:, core]),
                (ds_hbm, dse.at[:, core]),
                (lab_hbm, labe.at[rows : 2 * rows]),
                (mask_hbm, maske.at[rows : 2 * rows]),
            ]
        )
    ]
    for copy in local:
        copy.start()

    barrier = pltpu.get_barrier_semaphore()

    def greet(tt, dd):
        pl.semaphore_signal(barrier, inc=1, device_id=(tt, dd), device_id_type=MESH)

    for n in range(1, nd):
        greet(t, lax.rem(d + n, nd))

    @pl.when(has_above)
    def _():
        for n in range(nd):
            greet(above, n)

    @pl.when(has_below)
    def _():
        for n in range(nd):
            greet(below, n)

    beside_count = jnp.where(has_above, 1, 0) + jnp.where(has_below, 1, 0)
    pl.semaphore_wait(barrier, nd - 1 + nd * beside_count)

    number = [0]

    def remote(src, dst, tt, dd):
        n = number[0]
        number[0] = n + 1
        return pltpu.make_async_remote_copy(
            src_ref=src,
            dst_ref=dst,
            send_sem=send_sem.at[n],
            recv_sem=recv_sem.at[n],
            device_id=(tt, dd),
            device_id_type=MESH,
        )

    top, bottom = 2 + rows, 1
    first, last = slice(0, 8), slice(depth - 8, depth)
    after, before = slice(end, end + 8), slice(PAD - 8, PAD)
    pairs = [(p_hbm, pe), (s_hbm, se)]
    to_right = [remote(a.at[:, last], b.at[core_rows, before], t, right) for a, b in pairs]
    to_left = [remote(a.at[:, first], b.at[core_rows, after], t, left) for a, b in pairs]
    for a, b in [(dp_hbm, dpe), (ds_hbm, dse)]:
        to_right.append(remote(a.at[:, last], b.at[:, before], t, right))
        to_left.append(remote(a.at[:, first], b.at[:, after], t, left))
    diagonals = []
    for tt, going_t, coming_t, src_row, dst_row in [
        (above, has_above, has_below, rows - 1, bottom),
        (below, has_below, has_above, 0, top),
    ]:
        for dd, going_d, coming_d, src_k, dst_k in [
            (right, has_right, has_left, last, before),
            (left, has_left, has_right, first, after),
        ]:
            copies = [
                remote(a.at[pl.ds(src_row, 1), src_k], b.at[pl.ds(dst_row, 1), dst_k], tt, dd)
                for a, b in pairs
            ]
            diagonals.append((going_t & going_d, coming_t & coming_d, copies, dst_row, dst_k))
    up_near = [remote(lab_hbm, labe.at[0:rows], above, d), remote(mask_hbm, maske.at[0:rows], above, d)]
    down_near = [
        remote(lab_hbm, labe.at[2 * rows : 3 * rows], below, d),
        remote(mask_hbm, maske.at[2 * rows : 3 * rows], below, d),
    ]
    for a, b in pairs:
        up_near.append(remote(a.at[pl.ds(rows - 1, 1)], b.at[pl.ds(1, 1), core], above, d))
        down_near.append(remote(a.at[pl.ds(0, 1)], b.at[pl.ds(top, 1), core], below, d))
    up_far = [remote(a.at[pl.ds(rows - 2, 1)], b.at[pl.ds(0, 1), core], above, d) for a, b in pairs]
    down_far = [remote(a.at[pl.ds(1, 1)], b.at[pl.ds(top + 1, 1), core], below, d) for a, b in pairs]

    def start(condition, copies):
        @pl.when(condition)
        def _():
            for copy in copies:
                copy.start()

    def arrive(condition, copies):
        @pl.when(condition)
        def _():
            for copy in copies:
                copy.wait_recv()

    def sent(condition, copies):
        @pl.when(condition)
        def _():
            for copy in copies:
                copy.wait_send()

    start(has_above, up_near)
    start(has_below, down_near)
    start(has_right, to_right)
    start(has_left, to_left)
    for going, coming, copies, _, _ in diagonals:
        start(going, copies)
    start(has_above, up_far)
    start(has_below, down_far)

    row_zero = jnp.zeros((depth, cols), jnp.float32)
    tile_zero = jnp.zeros((8, cols), jnp.float32)
    label_zero = jnp.zeros((rows, cols), jnp.int32)

    def no_row(condition, near, far, label_at):
        @pl.when(jnp.logical_not(condition))
        def _():
            for b in (pe, se):
                b[near, core] = row_zero
                b[far, core] = row_zero
            labe[label_at : label_at + rows] = label_zero
            maske[label_at : label_at + rows] = label_zero

    no_row(has_below, 1, 0, 0)
    no_row(has_above, top, top + 1, 2 * rows)

    def no_side(condition, span):
        @pl.when(jnp.logical_not(condition))
        def _():
            for r in range(rows):
                pe[2 + r, span] = tile_zero
                se[2 + r, span] = tile_zero
                dpe[r, span] = tile_zero
                dse[r, span] = tile_zero

    no_side(has_left, before)
    no_side(has_right, after)
    for _, coming, _, dst_row, dst_k in diagonals:

        @pl.when(jnp.logical_not(coming))
        def _():
            pe[dst_row, dst_k] = tile_zero
            se[dst_row, dst_k] = tile_zero

    for copy in local:
        copy.wait()

    def set_growth(j):
        row = labe[rows - 1 + j : rows + j]
        growb[j] = jnp.broadcast_to(growth(row), (8, cols))

    for j in range(1, rows + 1):
        set_growth(j)

    sub = lax.broadcasted_iota(jnp.int32, (CH, cols), 0)
    low_end = jnp.where(d == 0, PAD, -1)
    high_end = jnp.where(d == nd - 1, end - 1, -1)

    def spread(ref, r, k0):
        block = ref[r, pl.ds(pl.multiple_of(k0 - 8, 8), CH + 16), :]
        size = CH + 16
        beside = pltpu.roll(block, 1, 0) + pltpu.roll(block, size - 1, 0)
        center = block[8 : 8 + CH]
        return center, beside[8 : 8 + CH] + lanes(center) - 6.0 * center

    def at(ref, r, k0):
        return ref[r, pl.ds(pl.multiple_of(k0, 8), CH), :]

    def base_next(i, k0, grow):
        p, lap_p = spread(pe, i, k0)
        s, lap_s = spread(se, i, k0)
        lap_p = lap_p + at(pe, i - 1, k0) + at(pe, i + 1, k0)
        lap_s = lap_s + at(se, i - 1, k0) + at(se, i + 1, k0)
        shell = 1.0 - p * p
        p_next = p + 0.1 * (lap_p + grow * (p - p * p * p) - shell * shell * s)
        s_next = s + 0.1 * lap_s + 0.5 * (p_next - p)
        return p, s, p_next, s_next

    def save_slopes(i, k0, slope_p, slope_s, at_end):
        span = pl.ds(pl.multiple_of(k0, 8), CH)
        c1[i - 1, span, :] = 0.05 * slope_p + 0.025 * slope_s - 0.1 * at_end
        a1[i - 1, span, :] = 0.05 * slope_s - 0.1 * at_end

    def ends_of(k0):
        k = sub + k0
        at_end = jnp.where((k == low_end) | (k == high_end), 1.0, 0.0)
        inside = (k >= PAD) & (k < end)
        return at_end, inside

    chunks = (depth + 16) // CH

    def own_row(i, has_lower, has_upper):
        j = i - 2
        grow = tiles(growb[i - 1], CH // 8)

        def one(n, carry):
            k0 = PAD - 8 + n * CH
            at_end, inside = ends_of(k0)
            p, s, p1, s1 = base_next(i, k0, grow)
            slope_p, slope_s = slopes(p, s, grow)
            span = pl.ds(pl.multiple_of(k0, 8), CH)
            wide[j, span, :] = 0.4 + 0.1 * slope_p
            solw[j, span, :] = 0.1 * slope_s
            next_p, next_s = slopes(p1, s1, grow)
            save_slopes(i, k0, next_p, next_s, at_end)
            dp, lap_dp = spread(dpe, j, k0)
            ds, lap_ds = spread(dse, j, k0)
            if has_lower:
                lap_dp = lap_dp + at(dpe, j - 1, k0)
                lap_ds = lap_ds + at(dse, j - 1, k0)
            if has_upper:
                lap_dp = lap_dp + at(dpe, j + 1, k0)
                lap_ds = lap_ds + at(dse, j + 1, k0)
            dp1 = dp + 0.1 * (lap_dp + slope_p * dp + slope_s * ds)
            ds1 = ds + 0.1 * lap_ds + 0.5 * (dp1 - dp)
            weight = 4.0 + at_end
            blend = 0.1 * s1 + 0.05 * p1
            dblend = 0.1 * ds1 + 0.05 * dp1
            term = s1 + 0.05 * (grow * (p1 - p1 * p1 * p1) + next_s * s1) - weight * blend
            dterm = ds1 + 0.05 * (next_p * dp1 + next_s * ds1) - weight * dblend
            parts = (term, blend, dterm, dblend)
            return tuple(c + fold(jnp.where(inside, v, 0.0)) for c, v in zip(carry, parts))

        zero = jnp.zeros((8, cols), jnp.float32)
        sums = lax.fori_loop(0, chunks, one, (zero, zero, zero, zero))
        for q in range(4):
            accs[q, j] = sums[q]

    def halo_row(i, j, slot):
        grow = tiles(growb[i - 1], CH // 8)

        def one(n, carry):
            k0 = PAD - 8 + n * CH
            at_end, inside = ends_of(k0)
            _, _, p1, s1 = base_next(i, k0, grow)
            next_p, next_s = slopes(p1, s1, grow)
            save_slopes(i, k0, next_p, next_s, at_end)
            dp, ds = at(dpe, j, k0), at(dse, j, k0)
            add_p = 0.1 * dp
            add_s = 0.1 * ds + 0.05 * dp
            dblend = 0.1 * add_s + 0.05 * add_p
            dterm = add_s + 0.05 * (next_p * add_p + next_s * add_s) - (4.0 + at_end) * dblend
            return tuple(
                c + fold(jnp.where(inside, v, 0.0)) for c, v in zip(carry, (dterm, dblend))
            )

        zero = jnp.zeros((8, cols), jnp.float32)
        sums = lax.fori_loop(0, chunks, one, (zero, zero))
        cross[slot] = sums[0]
        cross[slot + 1] = sums[1]

    def no_halo_row(i, slot):
        c1[i - 1] = jnp.zeros((end + PAD, cols), jnp.float32)
        a1[i - 1] = jnp.zeros((end + PAD, cols), jnp.float32)
        cross[slot] = tile_zero
        cross[slot + 1] = tile_zero

    arrive(has_left, to_right)
    arrive(has_right, to_left)

    def middle(i, carry):
        own_row(i, True, True)
        return carry

    lax.fori_loop(3, rows + 1, middle, 0)
    for _, coming, copies, _, _ in diagonals:
        arrive(coming, copies)
    arrive(has_below, up_near)
    arrive(has_above, down_near)
    set_growth(0)
    set_growth(rows + 1)
    own_row(2, False, True)
    own_row(rows + 1, True, False)

    arrive(has_below, up_far)
    arrive(has_above, down_far)

    @pl.when(has_below)
    def _():
        halo_row(1, 0, 0)

    @pl.when(jnp.logical_not(has_below))
    def _():
        no_halo_row(1, 0)

    @pl.when(has_above)
    def _():
        halo_row(rows + 2, rows - 1, 2)

    @pl.when(jnp.logical_not(has_above))
    def _():
        no_halo_row(rows + 2, 2)

    place = lax.broadcasted_iota(jnp.int32, (rows, cols), 0)

    def beside_rows(x):
        return jnp.where(place == 0, 0.0, pltpu.roll(x, 1, 0)) + jnp.where(
            place == rows - 1, 0.0, pltpu.roll(x, rows - 1, 0)
        )

    term, blend, dterm, dblend = [jnp.sum(accs[q], axis=1) for q in range(4)]
    x_low, q_low, x_high, q_high = [jnp.sum(cross[q], axis=0, keepdims=True) for q in range(4)]
    own_s = term + lanes(blend) + beside_rows(blend)
    own_d = dterm + lanes(dblend) + beside_rows(dblend)
    own_d = own_d + jnp.where(place == 0, q_low, 0.0) + jnp.where(place == rows - 1, q_high, 0.0)
    low_d = dblend[0:1] + x_low + lanes(q_low)
    high_d = dblend[rows - 1 : rows] + x_high + lanes(q_high)
    line = jnp.zeros((1, cols), jnp.float32)
    own_out[0:rows] = own_s
    own_out[rows : 2 * rows] = own_d
    tail = 2 * rows
    halo = [line, blend[0:1], blend[rows - 1 : rows], line, q_low, low_d, high_d, q_high]
    for n, value in enumerate(halo):
        own_out[tail + n : tail + n + 1] = value
    up_out[0:2] = own_s[rows - 2 : rows]
    up_out[2:3] = halo[2]
    up_out[3:4] = line
    up_out[4:6] = own_d[rows - 2 : rows]
    up_out[6:7] = high_d
    up_out[7:8] = q_high
    down_out[0:1] = line
    down_out[1:2] = halo[1]
    down_out[2:4] = own_s[0:2]
    down_out[4:5] = q_low
    down_out[5:6] = low_d
    down_out[6:8] = own_d[0:2]

    def message(src, inbox, sends, receives, n, slot, tt, dd):
        return pltpu.make_async_remote_copy(
            src_ref=src,
            dst_ref=inbox.at[slot],
            send_sem=sends.at[n],
            recv_sem=receives.at[slot],
            device_id=(tt, dd),
            device_id_type=MESH,
        )

    own_messages = [
        message(own_out, own_in, own_send, own_recv, n - 1, d, t, lax.rem(d + n, nd))
        for n in range(1, nd)
    ]
    up_messages = [message(up_out, up_in, up_send, up_recv, n, d, above, n) for n in range(nd)]
    down_messages = [
        message(down_out, down_in, down_send, down_recv, n, d, below, n) for n in range(nd)
    ]
    start(has_above, up_messages)
    start(has_below, down_messages)
    for copy in own_messages:
        copy.start()
    own_in[d] = own_out[...]

    @pl.when(jnp.logical_not(has_below))
    def _():
        for n in range(nd):
            up_in[n] = tile_zero

    @pl.when(jnp.logical_not(has_above))
    def _():
        for n in range(nd):
            down_in[n] = tile_zero

    ext[...] = jnp.zeros_like(ext)
    for n in range(1, nd):
        slot = lax.rem(d + n, nd)
        message(own_out, own_in, own_send, own_recv, n - 1, slot, t, slot).wait_recv()

    @pl.when(has_below)
    def _():
        for n in range(nd):
            message(up_out, up_in, up_send, up_recv, n, n, above, n).wait_recv()

    @pl.when(has_above)
    def _():
        for n in range(nd):
            message(down_out, down_in, down_send, down_recv, n, n, below, n).wait_recv()

    total, low, high = own_in[0], up_in[0], down_in[0]
    for n in range(1, nd):
        total, low, high = total + own_in[n], low + up_in[n], high + down_in[n]
    for q in range(2):
        ext[q, 0:2] = total[tail + 4 * q : tail + 4 * q + 2] + low[4 * q : 4 * q + 2]
        ext[q, 2 : 2 + rows] = total[q * rows : (q + 1) * rows]
        ext[q, 2:4] += low[4 * q + 2 : 4 * q + 4]
        ext[q, rows : rows + 2] += high[4 * q : 4 * q + 2]
        ext[q, rows + 2 : rows + 4] = (
            total[tail + 4 * q + 2 : tail + 4 * q + 4] + high[4 * q + 2 : 4 * q + 4]
        )
    root = math.sqrt(depth * nd)
    high_rows = ext.shape[1]
    bright = jnp.exp(-ext[0] / root)
    change = -bright * ext[1] / root
    mask = maske[rows - 2 : rows - 2 + high_rows].astype(jnp.float32)
    where = lax.broadcasted_iota(jnp.int32, (high_rows, cols), 0)
    valid = jnp.where(has_below, 0, 2)
    valid_end = jnp.where(has_above, rows + 4, rows + 2)
    inside_rows = (where >= valid) & (where < valid_end)
    back = jnp.where(inside_rows, -bright * mask * change, 0.0)
    change_ref[...] = change[2 : 2 + rows]
    flat = pltpu.roll(back, 1, 0) + pltpu.roll(back, high_rows - 1, 0) + lanes(back) - 4.0 * back
    flat = jnp.where(inside_rows, flat, 0.0)
    g = 0.5 * back + 0.1 * flat
    h = back + 0.1 * flat
    for j in range(rows + 2):
        bb[j] = jnp.broadcast_to(back[j + 1 : j + 2], (8, cols))
        gb[j] = jnp.broadcast_to(g[j + 1 : j + 2], (8, cols))
        hb[j] = jnp.broadcast_to(h[j + 1 : j + 2], (8, cols))

    def carry_row(j, carry):
        b, gg, hh = [tiles(x[j], CH // 8) for x in (bb, gb, hb)]
        for n in range(chunks):
            span = slice(PAD - 8 + n * CH, PAD - 8 + (n + 1) * CH)
            c1[j, span] = gg + c1[j, span] * b
            a1[j, span] = hh + a1[j, span] * b
        return carry

    lax.fori_loop(0, rows + 2, carry_row, 0)

    def no_depth(condition, span):
        @pl.when(jnp.logical_not(condition))
        def _():
            for j in range(rows + 2):
                c1[j, span] = tile_zero
                a1[j, span] = tile_zero

    no_depth(has_left, before)
    no_depth(has_right, after)

    def near(ref, j, k0):
        size = BC + 16
        block = ref[j, k0 - 8 : k0 - 8 + size]
        beside = pltpu.roll(block, 1, 0) + pltpu.roll(block, size - 1, 0)
        center = block[8 : 8 + BC]
        span = slice(k0, k0 + BC)
        return center, beside[8 : 8 + BC] + lanes(center) + ref[j - 1, span] + ref[j + 1, span]

    def out_copies(j):
        return [
            pltpu.make_async_copy(hp.at[j], hp_hbm.at[j], out_sem.at[0, j]),
            pltpu.make_async_copy(hs.at[j], hs_hbm.at[j], out_sem.at[1, j]),
        ]

    def finish(j, carry):
        for n in range(depth // BC):
            k0 = PAD + n * BC
            c, near_c = near(c1, j + 1, k0)
            a, near_a = near(a1, j + 1, k0)
            span = slice(k0, k0 + BC)
            dst = slice(n * BC, (n + 1) * BC)
            hp[j, dst] = c * wide[j, span] + 0.1 * near_c - 0.5 * a
            hs[j, dst] = 0.4 * a + 0.1 * near_a + solw[j, span] * c
        for copy in out_copies(j):
            copy.start()
        return carry

    lax.fori_loop(0, rows, finish, 0)
    for copy in own_messages:
        copy.wait_send()
    sent(has_above, up_messages + up_near + up_far)
    sent(has_below, down_messages + down_near + down_far)
    sent(has_right, to_right)
    sent(has_left, to_left)
    for going, coming, copies, _, _ in diagonals:
        sent(going, copies)
    for j in range(rows):
        for copy in out_copies(j):
            copy.wait()


def local(nt, nd, phase, solute, dphase, dsolute, labels, pixel_mask):
    rows, depth, cols = phase.shape
    f32, i32 = jnp.float32, jnp.int32
    length = depth + 2 * PAD
    dma = pltpu.SemaphoreType.DMA
    any_space = pl.BlockSpec(memory_space=pl.ANY)
    vmem = pl.BlockSpec(memory_space=pltpu.VMEM)
    field = jax.ShapeDtypeStruct((rows, depth, cols), f32)
    return pl.pallas_call(
        functools.partial(kernel, nt, nd),
        out_shape=(field, field, jax.ShapeDtypeStruct((rows, cols), f32)),
        in_specs=[any_space] * 6,
        out_specs=(any_space, any_space, vmem),
        scratch_shapes=[
            pltpu.VMEM((rows + 4, length, cols), f32),
            pltpu.VMEM((rows + 4, length, cols), f32),
            pltpu.VMEM((rows, length, cols), f32),
            pltpu.VMEM((rows, length, cols), f32),
            pltpu.VMEM((3 * rows, cols), i32),
            pltpu.VMEM((3 * rows, cols), i32),
            pltpu.VMEM((rows + 2, 8, cols), f32),
            pltpu.VMEM((rows + 2, length, cols), f32),
            pltpu.VMEM((rows + 2, length, cols), f32),
            pltpu.VMEM((rows, length, cols), f32),
            pltpu.VMEM((rows, length, cols), f32),
            pltpu.VMEM((rows, depth, cols), f32),
            pltpu.VMEM((rows, depth, cols), f32),
            pltpu.VMEM((4, rows, 8, cols), f32),
            pltpu.VMEM((4, 8, cols), f32),
            pltpu.VMEM((2 * rows + 8, cols), f32),
            pltpu.VMEM((8, cols), f32),
            pltpu.VMEM((8, cols), f32),
            pltpu.VMEM((nd, 2 * rows + 8, cols), f32),
            pltpu.VMEM((nd, 8, cols), f32),
            pltpu.VMEM((nd, 8, cols), f32),
            pltpu.VMEM((2, rows + 8, cols), f32),
            pltpu.VMEM((rows + 2, 8, cols), f32),
            pltpu.VMEM((rows + 2, 8, cols), f32),
            pltpu.VMEM((rows + 2, 8, cols), f32),
            dma((6,)),
            dma((2, rows)),
            dma((28,)),
            dma((28,)),
            dma((nd - 1,)),
            dma((nd,)),
            dma((nd,)),
            dma((nd,)),
            dma((nd,)),
            dma((nd,)),
        ],
        compiler_params=pltpu.CompilerParams(
            collective_id=0, has_side_effects=True, vmem_limit_bytes=63 * 1024 * 1024
        ),
    )(phase, solute, dphase, dsolute, labels, pixel_mask)


def solution(mesh):
    field, plane = P("tile", "depth", None), P("tile", None)
    return jax.shard_map(
        functools.partial(local, mesh.shape["tile"], mesh.shape["depth"]),
        mesh=mesh,
        in_specs=(field, field, field, field, plane, plane),
        out_specs=(field, field, plane),
        check_vma=False,
    )
```

```python
import functools
import math

import jax
import jax.numpy as jnp
from jax import lax
from jax.experimental import pallas as pl
from jax.experimental.pallas import tpu as pltpu
from jax.sharding import PartitionSpec as P

MESH = pl.DeviceIdType.MESH
PAD = 16
CH = 48
BC = 32


def growth(labels):
    return jnp.where(
        labels == 0, 0.6, jnp.where(labels == 1, 1.0, jnp.where(labels == 2, 1.7, 0.8))
    ).astype(jnp.float32)


def slopes(p, s, grow):
    shell = 1.0 - p * p
    return grow * (1.0 - 3.0 * p * p) + 4.0 * p * shell * s, -shell * shell


def tiles(block, count):
    return jnp.concatenate([block] * count, axis=0)


def fold(value):
    total = value[0:8]
    for k in range(8, value.shape[0], 8):
        total = total + value[k : k + 8]
    return total


def lanes(value):
    cols = value.shape[1]
    lane = lax.broadcasted_iota(jnp.int32, value.shape, 1)
    left = jnp.where(lane == 0, 0.0, pltpu.roll(value, 1, 1))
    right = jnp.where(lane == cols - 1, 0.0, pltpu.roll(value, cols - 1, 1))
    return left + right


def kernel(
    nt, nd,
    p_hbm, s_hbm, dp_hbm, ds_hbm, lab_hbm, mask_hbm,
    hp_hbm, hs_hbm, change_ref,
    pe, se, dpe, dse, labe, maske, growb,
    c1, a1, wide, solw, hp, hs,
    accs, cross, own_out, up_out, down_out, own_in, up_in, down_in,
    ext, bb, gb, hb,
    local_sem, out_sem, send_sem, recv_sem, own_send, own_recv, up_send, up_recv, down_send, down_recv,
):
    rows, depth, cols = p_hbm.shape
    t = lax.axis_index("tile")
    d = lax.axis_index("depth")
    has_above, has_below = t < nt - 1, t > 0
    has_right, has_left = d < nd - 1, d > 0
    above, below = lax.rem(t + 1, nt), lax.rem(t + nt - 1, nt)
    right, left = lax.rem(d + 1, nd), lax.rem(d + nd - 1, nd)
    end = PAD + depth
    core = slice(PAD, end)
    core_rows = slice(2, 2 + rows)

    local = [
        pltpu.make_async_copy(src, dst, local_sem.at[n])
        for n, (src, dst) in enumerate(
            [
                (p_hbm, pe.at[core_rows, core]),
                (s_hbm, se.at[core_rows, core]),
                (dp_hbm, dpe.at[:, core]),
                (ds_hbm, dse.at[:, core]),
                (lab_hbm, labe.at[rows : 2 * rows]),
                (mask_hbm, maske.at[rows : 2 * rows]),
            ]
        )
    ]
    for copy in local:
        copy.start()

    barrier = pltpu.get_barrier_semaphore()

    def greet(tt, dd):
        pl.semaphore_signal(barrier, inc=1, device_id=(tt, dd), device_id_type=MESH)

    for n in range(1, nd):
        greet(t, lax.rem(d + n, nd))

    @pl.when(has_above)
    def _():
        for n in range(nd):
            greet(above, n)

    @pl.when(has_below)
    def _():
        for n in range(nd):
            greet(below, n)

    beside_count = jnp.where(has_above, 1, 0) + jnp.where(has_below, 1, 0)
    pl.semaphore_wait(barrier, nd - 1 + nd * beside_count)

    number = [0]

    def remote(src, dst, tt, dd):
        n = number[0]
        number[0] = n + 1
        return pltpu.make_async_remote_copy(
            src_ref=src,
            dst_ref=dst,
            send_sem=send_sem.at[n],
            recv_sem=recv_sem.at[n],
            device_id=(tt, dd),
            device_id_type=MESH,
        )

    top, bottom = 2 + rows, 1
    first, last = slice(0, 8), slice(depth - 8, depth)
    after, before = slice(end, end + 8), slice(PAD - 8, PAD)
    pairs = [(p_hbm, pe), (s_hbm, se)]
    to_right = [remote(a.at[:, last], b.at[core_rows, before], t, right) for a, b in pairs]
    to_left = [remote(a.at[:, first], b.at[core_rows, after], t, left) for a, b in pairs]
    for a, b in [(dp_hbm, dpe), (ds_hbm, dse)]:
        to_right.append(remote(a.at[:, last], b.at[:, before], t, right))
        to_left.append(remote(a.at[:, first], b.at[:, after], t, left))
    diagonals = []
    for tt, going_t, coming_t, src_row, dst_row in [
        (above, has_above, has_below, rows - 1, bottom),
        (below, has_below, has_above, 0, top),
    ]:
        for dd, going_d, coming_d, src_k, dst_k in [
            (right, has_right, has_left, last, before),
            (left, has_left, has_right, first, after),
        ]:
            copies = [
                remote(a.at[pl.ds(src_row, 1), src_k], b.at[pl.ds(dst_row, 1), dst_k], tt, dd)
                for a, b in pairs
            ]
            diagonals.append((going_t & going_d, coming_t & coming_d, copies, dst_row, dst_k))
    up_near = [remote(lab_hbm, labe.at[0:rows], above, d), remote(mask_hbm, maske.at[0:rows], above, d)]
    down_near = [
        remote(lab_hbm, labe.at[2 * rows : 3 * rows], below, d),
        remote(mask_hbm, maske.at[2 * rows : 3 * rows], below, d),
    ]
    for a, b in pairs:
        up_near.append(remote(a.at[pl.ds(rows - 1, 1)], b.at[pl.ds(1, 1), core], above, d))
        down_near.append(remote(a.at[pl.ds(0, 1)], b.at[pl.ds(top, 1), core], below, d))
    up_far = [remote(a.at[pl.ds(rows - 2, 1)], b.at[pl.ds(0, 1), core], above, d) for a, b in pairs]
    down_far = [remote(a.at[pl.ds(1, 1)], b.at[pl.ds(top + 1, 1), core], below, d) for a, b in pairs]

    def start(condition, copies):
        @pl.when(condition)
        def _():
            for copy in copies:
                copy.start()

    def arrive(condition, copies):
        @pl.when(condition)
        def _():
            for copy in copies:
                copy.wait_recv()

    def sent(condition, copies):
        @pl.when(condition)
        def _():
            for copy in copies:
                copy.wait_send()

    start(has_above, up_near)
    start(has_below, down_near)
    start(has_right, to_right)
    start(has_left, to_left)
    for going, coming, copies, _, _ in diagonals:
        start(going, copies)

    row_zero = jnp.zeros((depth, cols), jnp.float32)
    tile_zero = jnp.zeros((8, cols), jnp.float32)
    label_zero = jnp.zeros((rows, cols), jnp.int32)

    def no_row(condition, near, far, label_at):
        @pl.when(jnp.logical_not(condition))
        def _():
            for b in (pe, se):
                b[near, core] = row_zero
                b[far, core] = row_zero
            labe[label_at : label_at + rows] = label_zero
            maske[label_at : label_at + rows] = label_zero

    no_row(has_below, 1, 0, 0)
    no_row(has_above, top, top + 1, 2 * rows)

    def no_side(condition, span):
        @pl.when(jnp.logical_not(condition))
        def _():
            for r in range(rows):
                pe[2 + r, span] = tile_zero
                se[2 + r, span] = tile_zero
                dpe[r, span] = tile_zero
                dse[r, span] = tile_zero

    no_side(has_left, before)
    no_side(has_right, after)
    for _, coming, _, dst_row, dst_k in diagonals:

        @pl.when(jnp.logical_not(coming))
        def _():
            pe[dst_row, dst_k] = tile_zero
            se[dst_row, dst_k] = tile_zero

    for copy in local:
        copy.wait()

    def set_growth(j):
        row = labe[rows - 1 + j : rows + j]
        growb[j] = jnp.broadcast_to(growth(row), (8, cols))

    for j in range(1, rows + 1):
        set_growth(j)

    sub = lax.broadcasted_iota(jnp.int32, (CH, cols), 0)
    low_end = jnp.where(d == 0, PAD, -1)
    high_end = jnp.where(d == nd - 1, end - 1, -1)

    def spread(ref, r, k0):
        block = ref[r, pl.ds(pl.multiple_of(k0 - 8, 8), CH + 16), :]
        size = CH + 16
        beside = pltpu.roll(block, 1, 0) + pltpu.roll(block, size - 1, 0)
        center = block[8 : 8 + CH]
        return center, beside[8 : 8 + CH] + lanes(center) - 6.0 * center

    def at(ref, r, k0):
        return ref[r, pl.ds(pl.multiple_of(k0, 8), CH), :]

    def base_next(i, k0, grow):
        p, lap_p = spread(pe, i, k0)
        s, lap_s = spread(se, i, k0)
        lap_p = lap_p + at(pe, i - 1, k0) + at(pe, i + 1, k0)
        lap_s = lap_s + at(se, i - 1, k0) + at(se, i + 1, k0)
        shell = 1.0 - p * p
        p_next = p + 0.1 * (lap_p + grow * (p - p * p * p) - shell * shell * s)
        s_next = s + 0.1 * lap_s + 0.5 * (p_next - p)
        return p, s, p_next, s_next

    def save_slopes(i, k0, slope_p, slope_s, at_end):
        span = pl.ds(pl.multiple_of(k0, 8), CH)
        c1[i - 1, span, :] = 0.05 * slope_p + 0.025 * slope_s - 0.1 * at_end
        a1[i - 1, span, :] = 0.05 * slope_s - 0.1 * at_end

    def ends_of(k0):
        k = sub + k0
        at_end = jnp.where((k == low_end) | (k == high_end), 1.0, 0.0)
        inside = (k >= PAD) & (k < end)
        return at_end, inside

    chunks = (depth + 16) // CH

    def own_row(i, has_lower, has_upper):
        j = i - 2
        grow = tiles(growb[i - 1], CH // 8)

        def one(n, carry):
            k0 = PAD - 8 + n * CH
            at_end, inside = ends_of(k0)
            p, s, p1, s1 = base_next(i, k0, grow)
            slope_p, slope_s = slopes(p, s, grow)
            span = pl.ds(pl.multiple_of(k0, 8), CH)
            wide[j, span, :] = 0.4 + 0.1 * slope_p
            solw[j, span, :] = 0.1 * slope_s
            next_p, next_s = slopes(p1, s1, grow)
            save_slopes(i, k0, next_p, next_s, at_end)
            dp, lap_dp = spread(dpe, j, k0)
            ds, lap_ds = spread(dse, j, k0)
            if has_lower:
                lap_dp = lap_dp + at(dpe, j - 1, k0)
                lap_ds = lap_ds + at(dse, j - 1, k0)
            if has_upper:
                lap_dp = lap_dp + at(dpe, j + 1, k0)
                lap_ds = lap_ds + at(dse, j + 1, k0)
            dp1 = dp + 0.1 * (lap_dp + slope_p * dp + slope_s * ds)
            ds1 = ds + 0.1 * lap_ds + 0.5 * (dp1 - dp)
            weight = 4.0 + at_end
            blend = 0.1 * s1 + 0.05 * p1
            dblend = 0.1 * ds1 + 0.05 * dp1
            term = s1 + 0.05 * (grow * (p1 - p1 * p1 * p1) + next_s * s1) - weight * blend
            dterm = ds1 + 0.05 * (next_p * dp1 + next_s * ds1) - weight * dblend
            parts = (term, blend, dterm, dblend)
            return tuple(c + fold(jnp.where(inside, v, 0.0)) for c, v in zip(carry, parts))

        zero = jnp.zeros((8, cols), jnp.float32)
        sums = lax.fori_loop(0, chunks, one, (zero, zero, zero, zero))
        for q in range(4):
            accs[q, j] = sums[q]

    def halo_row(i, j, slot):
        grow = tiles(growb[i - 1], CH // 8)

        def one(n, carry):
            k0 = PAD - 8 + n * CH
            at_end, inside = ends_of(k0)
            _, _, p1, s1 = base_next(i, k0, grow)
            next_p, next_s = slopes(p1, s1, grow)
            save_slopes(i, k0, next_p, next_s, at_end)
            dp, ds = at(dpe, j, k0), at(dse, j, k0)
            add_p = 0.1 * dp
            add_s = 0.1 * ds + 0.05 * dp
            dblend = 0.1 * add_s + 0.05 * add_p
            dterm = add_s + 0.05 * (next_p * add_p + next_s * add_s) - (4.0 + at_end) * dblend
            return tuple(
                c + fold(jnp.where(inside, v, 0.0)) for c, v in zip(carry, (dterm, dblend))
            )

        zero = jnp.zeros((8, cols), jnp.float32)
        sums = lax.fori_loop(0, chunks, one, (zero, zero))
        cross[slot] = sums[0]
        cross[slot + 1] = sums[1]

    def no_halo_row(i, slot):
        c1[i - 1] = jnp.zeros((end + PAD, cols), jnp.float32)
        a1[i - 1] = jnp.zeros((end + PAD, cols), jnp.float32)
        cross[slot] = tile_zero
        cross[slot + 1] = tile_zero

    arrive(has_left, to_right)
    arrive(has_right, to_left)

    def middle(i, carry):
        own_row(i, True, True)
        return carry

    lax.fori_loop(3, rows + 1, middle, 0)
    start(has_above, up_far)
    start(has_below, down_far)
    for _, coming, copies, _, _ in diagonals:
        arrive(coming, copies)
    arrive(has_below, up_near)
    arrive(has_above, down_near)
    set_growth(0)
    set_growth(rows + 1)
    own_row(2, False, True)
    own_row(rows + 1, True, False)

    arrive(has_below, up_far)
    arrive(has_above, down_far)

    @pl.when(has_below)
    def _():
        halo_row(1, 0, 0)

    @pl.when(jnp.logical_not(has_below))
    def _():
        no_halo_row(1, 0)

    @pl.when(has_above)
    def _():
        halo_row(rows + 2, rows - 1, 2)

    @pl.when(jnp.logical_not(has_above))
    def _():
        no_halo_row(rows + 2, 2)

    place = lax.broadcasted_iota(jnp.int32, (rows, cols), 0)

    def beside_rows(x):
        return jnp.where(place == 0, 0.0, pltpu.roll(x, 1, 0)) + jnp.where(
            place == rows - 1, 0.0, pltpu.roll(x, rows - 1, 0)
        )

    term, blend, dterm, dblend = [jnp.sum(accs[q], axis=1) for q in range(4)]
    x_low, q_low, x_high, q_high = [jnp.sum(cross[q], axis=0, keepdims=True) for q in range(4)]
    own_s = term + lanes(blend) + beside_rows(blend)
    own_d = dterm + lanes(dblend) + beside_rows(dblend)
    own_d = own_d + jnp.where(place == 0, q_low, 0.0) + jnp.where(place == rows - 1, q_high, 0.0)
    low_d = dblend[0:1] + x_low + lanes(q_low)
    high_d = dblend[rows - 1 : rows] + x_high + lanes(q_high)
    line = jnp.zeros((1, cols), jnp.float32)
    own_out[0:rows] = own_s
    own_out[rows : 2 * rows] = own_d
    tail = 2 * rows
    halo = [line, blend[0:1], blend[rows - 1 : rows], line, q_low, low_d, high_d, q_high]
    for n, value in enumerate(halo):
        own_out[tail + n : tail + n + 1] = value
    up_out[0:2] = own_s[rows - 2 : rows]
    up_out[2:3] = halo[2]
    up_out[3:4] = line
    up_out[4:6] = own_d[rows - 2 : rows]
    up_out[6:7] = high_d
    up_out[7:8] = q_high
    down_out[0:1] = line
    down_out[1:2] = halo[1]
    down_out[2:4] = own_s[0:2]
    down_out[4:5] = q_low
    down_out[5:6] = low_d
    down_out[6:8] = own_d[0:2]

    def message(src, inbox, sends, receives, n, slot, tt, dd):
        return pltpu.make_async_remote_copy(
            src_ref=src,
            dst_ref=inbox.at[slot],
            send_sem=sends.at[n],
            recv_sem=receives.at[slot],
            device_id=(tt, dd),
            device_id_type=MESH,
        )

    own_messages = [
        message(own_out, own_in, own_send, own_recv, n - 1, d, t, lax.rem(d + n, nd))
        for n in range(1, nd)
    ]
    up_messages = [message(up_out, up_in, up_send, up_recv, n, d, above, n) for n in range(nd)]
    down_messages = [
        message(down_out, down_in, down_send, down_recv, n, d, below, n) for n in range(nd)
    ]
    start(has_above, up_messages)
    start(has_below, down_messages)
    for copy in own_messages:
        copy.start()
    own_in[d] = own_out[...]

    @pl.when(jnp.logical_not(has_below))
    def _():
        for n in range(nd):
            up_in[n] = tile_zero

    @pl.when(jnp.logical_not(has_above))
    def _():
        for n in range(nd):
            down_in[n] = tile_zero

    ext[...] = jnp.zeros_like(ext)
    for n in range(1, nd):
        slot = lax.rem(d + n, nd)
        message(own_out, own_in, own_send, own_recv, n - 1, slot, t, slot).wait_recv()

    @pl.when(has_below)
    def _():
        for n in range(nd):
            message(up_out, up_in, up_send, up_recv, n, n, above, n).wait_recv()

    @pl.when(has_above)
    def _():
        for n in range(nd):
            message(down_out, down_in, down_send, down_recv, n, n, below, n).wait_recv()

    total, low, high = own_in[0], up_in[0], down_in[0]
    for n in range(1, nd):
        total, low, high = total + own_in[n], low + up_in[n], high + down_in[n]
    for q in range(2):
        ext[q, 0:2] = total[tail + 4 * q : tail + 4 * q + 2] + low[4 * q : 4 * q + 2]
        ext[q, 2 : 2 + rows] = total[q * rows : (q + 1) * rows]
        ext[q, 2:4] += low[4 * q + 2 : 4 * q + 4]
        ext[q, rows : rows + 2] += high[4 * q : 4 * q + 2]
        ext[q, rows + 2 : rows + 4] = (
            total[tail + 4 * q + 2 : tail + 4 * q + 4] + high[4 * q + 2 : 4 * q + 4]
        )
    root = math.sqrt(depth * nd)
    high_rows = ext.shape[1]
    bright = jnp.exp(-ext[0] / root)
    change = -bright * ext[1] / root
    mask = maske[rows - 2 : rows - 2 + high_rows].astype(jnp.float32)
    where = lax.broadcasted_iota(jnp.int32, (high_rows, cols), 0)
    valid = jnp.where(has_below, 0, 2)
    valid_end = jnp.where(has_above, rows + 4, rows + 2)
    inside_rows = (where >= valid) & (where < valid_end)
    back = jnp.where(inside_rows, -bright * mask * change, 0.0)
    change_ref[...] = change[2 : 2 + rows]
    flat = pltpu.roll(back, 1, 0) + pltpu.roll(back, high_rows - 1, 0) + lanes(back) - 4.0 * back
    flat = jnp.where(inside_rows, flat, 0.0)
    g = 0.5 * back + 0.1 * flat
    h = back + 0.1 * flat
    for j in range(rows + 2):
        bb[j] = jnp.broadcast_to(back[j + 1 : j + 2], (8, cols))
        gb[j] = jnp.broadcast_to(g[j + 1 : j + 2], (8, cols))
        hb[j] = jnp.broadcast_to(h[j + 1 : j + 2], (8, cols))

    def carry_row(j, carry):
        b, gg, hh = [tiles(x[j], CH // 8) for x in (bb, gb, hb)]
        for n in range(chunks):
            span = slice(PAD - 8 + n * CH, PAD - 8 + (n + 1) * CH)
            c1[j, span] = gg + c1[j, span] * b
            a1[j, span] = hh + a1[j, span] * b
        return carry

    lax.fori_loop(0, rows + 2, carry_row, 0)

    def no_depth(condition, span):
        @pl.when(jnp.logical_not(condition))
        def _():
            for j in range(rows + 2):
                c1[j, span] = tile_zero
                a1[j, span] = tile_zero

    no_depth(has_left, before)
    no_depth(has_right, after)

    def near(ref, j, k0):
        size = BC + 16
        block = ref[j, k0 - 8 : k0 - 8 + size]
        beside = pltpu.roll(block, 1, 0) + pltpu.roll(block, size - 1, 0)
        center = block[8 : 8 + BC]
        span = slice(k0, k0 + BC)
        return center, beside[8 : 8 + BC] + lanes(center) + ref[j - 1, span] + ref[j + 1, span]

    def out_copies(j):
        return [
            pltpu.make_async_copy(hp.at[j], hp_hbm.at[j], out_sem.at[0, j]),
            pltpu.make_async_copy(hs.at[j], hs_hbm.at[j], out_sem.at[1, j]),
        ]

    def finish(j, carry):
        for n in range(depth // BC):
            k0 = PAD + n * BC
            c, near_c = near(c1, j + 1, k0)
            a, near_a = near(a1, j + 1, k0)
            span = slice(k0, k0 + BC)
            dst = slice(n * BC, (n + 1) * BC)
            hp[j, dst] = c * wide[j, span] + 0.1 * near_c - 0.5 * a
            hs[j, dst] = 0.4 * a + 0.1 * near_a + solw[j, span] * c
        for copy in out_copies(j):
            copy.start()
        return carry

    lax.fori_loop(0, rows, finish, 0)
    for copy in own_messages:
        copy.wait_send()
    sent(has_above, up_messages + up_near + up_far)
    sent(has_below, down_messages + down_near + down_far)
    sent(has_right, to_right)
    sent(has_left, to_left)
    for going, coming, copies, _, _ in diagonals:
        sent(going, copies)
    for j in range(rows):
        for copy in out_copies(j):
            copy.wait()


def local(nt, nd, phase, solute, dphase, dsolute, labels, pixel_mask):
    rows, depth, cols = phase.shape
    f32, i32 = jnp.float32, jnp.int32
    length = depth + 2 * PAD
    dma = pltpu.SemaphoreType.DMA
    any_space = pl.BlockSpec(memory_space=pl.ANY)
    vmem = pl.BlockSpec(memory_space=pltpu.VMEM)
    field = jax.ShapeDtypeStruct((rows, depth, cols), f32)
    return pl.pallas_call(
        functools.partial(kernel, nt, nd),
        out_shape=(field, field, jax.ShapeDtypeStruct((rows, cols), f32)),
        in_specs=[any_space] * 6,
        out_specs=(any_space, any_space, vmem),
        scratch_shapes=[
            pltpu.VMEM((rows + 4, length, cols), f32),
            pltpu.VMEM((rows + 4, length, cols), f32),
            pltpu.VMEM((rows, length, cols), f32),
            pltpu.VMEM((rows, length, cols), f32),
            pltpu.VMEM((3 * rows, cols), i32),
            pltpu.VMEM((3 * rows, cols), i32),
            pltpu.VMEM((rows + 2, 8, cols), f32),
            pltpu.VMEM((rows + 2, length, cols), f32),
            pltpu.VMEM((rows + 2, length, cols), f32),
            pltpu.VMEM((rows, length, cols), f32),
            pltpu.VMEM((rows, length, cols), f32),
            pltpu.VMEM((rows, depth, cols), f32),
            pltpu.VMEM((rows, depth, cols), f32),
            pltpu.VMEM((4, rows, 8, cols), f32),
            pltpu.VMEM((4, 8, cols), f32),
            pltpu.VMEM((2 * rows + 8, cols), f32),
            pltpu.VMEM((8, cols), f32),
            pltpu.VMEM((8, cols), f32),
            pltpu.VMEM((nd, 2 * rows + 8, cols), f32),
            pltpu.VMEM((nd, 8, cols), f32),
            pltpu.VMEM((nd, 8, cols), f32),
            pltpu.VMEM((2, rows + 8, cols), f32),
            pltpu.VMEM((rows + 2, 8, cols), f32),
            pltpu.VMEM((rows + 2, 8, cols), f32),
            pltpu.VMEM((rows + 2, 8, cols), f32),
            dma((6,)),
            dma((2, rows)),
            dma((28,)),
            dma((28,)),
            dma((nd - 1,)),
            dma((nd,)),
            dma((nd,)),
            dma((nd,)),
            dma((nd,)),
            dma((nd,)),
        ],
        compiler_params=pltpu.CompilerParams(
            collective_id=0, has_side_effects=True, vmem_limit_bytes=63 * 1024 * 1024
        ),
    )(phase, solute, dphase, dsolute, labels, pixel_mask)


def solution(mesh):
    field, plane = P("tile", "depth", None), P("tile", None)
    return jax.shard_map(
        functools.partial(local, mesh.shape["tile"], mesh.shape["depth"]),
        mesh=mesh,
        in_specs=(field, field, field, field, plane, plane),
        out_specs=(field, field, plane),
        check_vma=False,
    )
```

```python
import functools
import math

import jax
import jax.numpy as jnp
from jax import lax
from jax.experimental import pallas as pl
from jax.experimental.pallas import tpu as pltpu
from jax.sharding import PartitionSpec as P

MESH = pl.DeviceIdType.MESH
PAD = 16
CH = 48
BC = 32


def growth(labels):
    return jnp.where(
        labels == 0, 0.6, jnp.where(labels == 1, 1.0, jnp.where(labels == 2, 1.7, 0.8))
    ).astype(jnp.float32)


def slopes(p, s, grow):
    shell = 1.0 - p * p
    return grow * (1.0 - 3.0 * p * p) + 4.0 * p * shell * s, -shell * shell


def tiles(block, count):
    return jnp.concatenate([block] * count, axis=0)


def fold(value):
    total = value[0:8]
    for k in range(8, value.shape[0], 8):
        total = total + value[k : k + 8]
    return total


def lanes(value):
    cols = value.shape[1]
    lane = lax.broadcasted_iota(jnp.int32, value.shape, 1)
    left = jnp.where(lane == 0, 0.0, pltpu.roll(value, 1, 1))
    right = jnp.where(lane == cols - 1, 0.0, pltpu.roll(value, cols - 1, 1))
    return left + right


def kernel(
    nt, nd,
    p_hbm, s_hbm, dp_hbm, ds_hbm, lab_hbm, mask_hbm,
    hp_hbm, hs_hbm, change_ref,
    pe, se, dpe, dse, labe, maske, growb,
    c1, a1, wide, solw, hp, hs,
    accs, cross, own_out, up_out, down_out, own_in, up_in, down_in,
    ext, bb, gb, hb,
    local_sem, out_sem, send_sem, recv_sem, own_send, own_recv, up_send, up_recv, down_send, down_recv,
):
    rows, depth, cols = p_hbm.shape
    t = lax.axis_index("tile")
    d = lax.axis_index("depth")
    has_above, has_below = t < nt - 1, t > 0
    has_right, has_left = d < nd - 1, d > 0
    above, below = lax.rem(t + 1, nt), lax.rem(t + nt - 1, nt)
    right, left = lax.rem(d + 1, nd), lax.rem(d + nd - 1, nd)
    end = PAD + depth
    core = slice(PAD, end)
    core_rows = slice(2, 2 + rows)

    local = [
        pltpu.make_async_copy(src, dst, local_sem.at[n])
        for n, (src, dst) in enumerate(
            [
                (p_hbm, pe.at[core_rows, core]),
                (s_hbm, se.at[core_rows, core]),
                (dp_hbm, dpe.at[:, core]),
                (ds_hbm, dse.at[:, core]),
                (lab_hbm, labe.at[rows : 2 * rows]),
                (mask_hbm, maske.at[rows : 2 * rows]),
            ]
        )
    ]
    for copy in local:
        copy.start()

    barrier = pltpu.get_barrier_semaphore()

    def greet(tt, dd):
        pl.semaphore_signal(barrier, inc=1, device_id=(tt, dd), device_id_type=MESH)

    for n in range(1, nd):
        greet(t, lax.rem(d + n, nd))

    @pl.when(has_above)
    def _():
        for n in range(nd):
            greet(above, n)

    @pl.when(has_below)
    def _():
        for n in range(nd):
            greet(below, n)

    beside_count = jnp.where(has_above, 1, 0) + jnp.where(has_below, 1, 0)
    pl.semaphore_wait(barrier, nd - 1 + nd * beside_count)

    number = [0]

    def remote(src, dst, tt, dd):
        n = number[0]
        number[0] = n + 1
        return pltpu.make_async_remote_copy(
            src_ref=src,
            dst_ref=dst,
            send_sem=send_sem.at[n],
            recv_sem=recv_sem.at[n],
            device_id=(tt, dd),
            device_id_type=MESH,
        )

    top, bottom = 2 + rows, 1
    first, last = slice(0, 8), slice(depth - 8, depth)
    after, before = slice(end, end + 8), slice(PAD - 8, PAD)
    pairs = [(p_hbm, pe), (s_hbm, se)]
    to_right = [remote(a.at[:, last], b.at[core_rows, before], t, right) for a, b in pairs]
    to_left = [remote(a.at[:, first], b.at[core_rows, after], t, left) for a, b in pairs]
    for a, b in [(dp_hbm, dpe), (ds_hbm, dse)]:
        to_right.append(remote(a.at[:, last], b.at[:, before], t, right))
        to_left.append(remote(a.at[:, first], b.at[:, after], t, left))
    diagonals = []
    for tt, going_t, coming_t, src_row, dst_row in [
        (above, has_above, has_below, rows - 1, bottom),
        (below, has_below, has_above, 0, top),
    ]:
        for dd, going_d, coming_d, src_k, dst_k in [
            (right, has_right, has_left, last, before),
            (left, has_left, has_right, first, after),
        ]:
            copies = [
                remote(a.at[pl.ds(src_row, 1), src_k], b.at[pl.ds(dst_row, 1), dst_k], tt, dd)
                for a, b in pairs
            ]
            diagonals.append((going_t & going_d, coming_t & coming_d, copies, dst_row, dst_k))
    up_near = [remote(lab_hbm, labe.at[0:rows], above, d), remote(mask_hbm, maske.at[0:rows], above, d)]
    down_near = [
        remote(lab_hbm, labe.at[2 * rows : 3 * rows], below, d),
        remote(mask_hbm, maske.at[2 * rows : 3 * rows], below, d),
    ]
    for a, b in pairs:
        up_near.append(remote(a.at[pl.ds(rows - 1, 1)], b.at[pl.ds(1, 1), core], above, d))
        down_near.append(remote(a.at[pl.ds(0, 1)], b.at[pl.ds(top, 1), core], below, d))
    up_far = [remote(a.at[pl.ds(rows - 2, 1)], b.at[pl.ds(0, 1), core], above, d) for a, b in pairs]
    down_far = [remote(a.at[pl.ds(1, 1)], b.at[pl.ds(top + 1, 1), core], below, d) for a, b in pairs]

    def start(condition, copies):
        @pl.when(condition)
        def _():
            for copy in copies:
                copy.start()

    def arrive(condition, copies):
        @pl.when(condition)
        def _():
            for copy in copies:
                copy.wait_recv()

    def sent(condition, copies):
        @pl.when(condition)
        def _():
            for copy in copies:
                copy.wait_send()

    start(has_above, up_near)
    start(has_below, down_near)
    start(has_right, to_right)
    start(has_left, to_left)
    for going, coming, copies, _, _ in diagonals:
        start(going, copies)

    row_zero = jnp.zeros((depth, cols), jnp.float32)
    tile_zero = jnp.zeros((8, cols), jnp.float32)
    label_zero = jnp.zeros((rows, cols), jnp.int32)

    def no_row(condition, near, far, label_at):
        @pl.when(jnp.logical_not(condition))
        def _():
            for b in (pe, se):
                b[near, core] = row_zero
                b[far, core] = row_zero
            labe[label_at : label_at + rows] = label_zero
            maske[label_at : label_at + rows] = label_zero

    no_row(has_below, 1, 0, 0)
    no_row(has_above, top, top + 1, 2 * rows)

    def no_side(condition, span):
        @pl.when(jnp.logical_not(condition))
        def _():
            for r in range(rows):
                pe[2 + r, span] = tile_zero
                se[2 + r, span] = tile_zero
                dpe[r, span] = tile_zero
                dse[r, span] = tile_zero

    no_side(has_left, before)
    no_side(has_right, after)
    for _, coming, _, dst_row, dst_k in diagonals:

        @pl.when(jnp.logical_not(coming))
        def _():
            pe[dst_row, dst_k] = tile_zero
            se[dst_row, dst_k] = tile_zero

    for copy in local:
        copy.wait()

    def set_growth(j):
        row = labe[rows - 1 + j : rows + j]
        growb[j] = jnp.broadcast_to(growth(row), (8, cols))

    for j in range(1, rows + 1):
        set_growth(j)

    sub = lax.broadcasted_iota(jnp.int32, (CH, cols), 0)
    low_end = jnp.where(d == 0, PAD, -1)
    high_end = jnp.where(d == nd - 1, end - 1, -1)

    def spread(ref, r, k0):
        block = ref[r, pl.ds(pl.multiple_of(k0 - 8, 8), CH + 16), :]
        size = CH + 16
        beside = pltpu.roll(block, 1, 0) + pltpu.roll(block, size - 1, 0)
        center = block[8 : 8 + CH]
        return center, beside[8 : 8 + CH] + lanes(center) - 6.0 * center

    def at(ref, r, k0):
        return ref[r, pl.ds(pl.multiple_of(k0, 8), CH), :]

    def base_next(i, k0, grow):
        p, lap_p = spread(pe, i, k0)
        s, lap_s = spread(se, i, k0)
        lap_p = lap_p + at(pe, i - 1, k0) + at(pe, i + 1, k0)
        lap_s = lap_s + at(se, i - 1, k0) + at(se, i + 1, k0)
        shell = 1.0 - p * p
        p_next = p + 0.1 * (lap_p + grow * (p - p * p * p) - shell * shell * s)
        s_next = s + 0.1 * lap_s + 0.5 * (p_next - p)
        return p, s, p_next, s_next

    def save_slopes(i, k0, slope_p, slope_s, at_end):
        span = pl.ds(pl.multiple_of(k0, 8), CH)
        c1[i - 1, span, :] = 0.05 * slope_p + 0.025 * slope_s - 0.1 * at_end
        a1[i - 1, span, :] = 0.05 * slope_s - 0.1 * at_end

    def ends_of(k0):
        k = sub + k0
        at_end = jnp.where((k == low_end) | (k == high_end), 1.0, 0.0)
        inside = (k >= PAD) & (k < end)
        return at_end, inside

    chunks = (depth + 16) // CH

    def own_row(i, has_lower, has_upper):
        j = i - 2
        grow = tiles(growb[i - 1], CH // 8)

        def one(n, carry):
            k0 = PAD - 8 + n * CH
            at_end, inside = ends_of(k0)
            p, s, p1, s1 = base_next(i, k0, grow)
            slope_p, slope_s = slopes(p, s, grow)
            span = pl.ds(pl.multiple_of(k0, 8), CH)
            wide[j, span, :] = 0.4 + 0.1 * slope_p
            solw[j, span, :] = 0.1 * slope_s
            next_p, next_s = slopes(p1, s1, grow)
            save_slopes(i, k0, next_p, next_s, at_end)
            dp, lap_dp = spread(dpe, j, k0)
            ds, lap_ds = spread(dse, j, k0)
            if has_lower:
                lap_dp = lap_dp + at(dpe, j - 1, k0)
                lap_ds = lap_ds + at(dse, j - 1, k0)
            if has_upper:
                lap_dp = lap_dp + at(dpe, j + 1, k0)
                lap_ds = lap_ds + at(dse, j + 1, k0)
            dp1 = dp + 0.1 * (lap_dp + slope_p * dp + slope_s * ds)
            ds1 = ds + 0.1 * lap_ds + 0.5 * (dp1 - dp)
            weight = 4.0 + at_end
            blend = 0.1 * s1 + 0.05 * p1
            dblend = 0.1 * ds1 + 0.05 * dp1
            term = s1 + 0.05 * (grow * (p1 - p1 * p1 * p1) + next_s * s1) - weight * blend
            dterm = ds1 + 0.05 * (next_p * dp1 + next_s * ds1) - weight * dblend
            parts = (term, blend, dterm, dblend)
            return tuple(c + fold(jnp.where(inside, v, 0.0)) for c, v in zip(carry, parts))

        zero = jnp.zeros((8, cols), jnp.float32)
        sums = lax.fori_loop(0, chunks, one, (zero, zero, zero, zero))
        for q in range(4):
            accs[q, j] = sums[q]

    def halo_row(i, j, slot):
        grow = tiles(growb[i - 1], CH // 8)

        def one(n, carry):
            k0 = PAD - 8 + n * CH
            at_end, inside = ends_of(k0)
            _, _, p1, s1 = base_next(i, k0, grow)
            next_p, next_s = slopes(p1, s1, grow)
            save_slopes(i, k0, next_p, next_s, at_end)
            dp, ds = at(dpe, j, k0), at(dse, j, k0)
            add_p = 0.1 * dp
            add_s = 0.1 * ds + 0.05 * dp
            dblend = 0.1 * add_s + 0.05 * add_p
            dterm = add_s + 0.05 * (next_p * add_p + next_s * add_s) - (4.0 + at_end) * dblend
            return tuple(
                c + fold(jnp.where(inside, v, 0.0)) for c, v in zip(carry, (dterm, dblend))
            )

        zero = jnp.zeros((8, cols), jnp.float32)
        sums = lax.fori_loop(0, chunks, one, (zero, zero))
        cross[slot] = sums[0]
        cross[slot + 1] = sums[1]

    def no_halo_row(i, slot):
        c1[i - 1] = jnp.zeros((end + PAD, cols), jnp.float32)
        a1[i - 1] = jnp.zeros((end + PAD, cols), jnp.float32)
        cross[slot] = tile_zero
        cross[slot + 1] = tile_zero

    arrive(has_left, to_right)
    arrive(has_right, to_left)

    def middle(i, carry):
        own_row(i, True, True)
        return carry

    lax.fori_loop(3, rows + 1, middle, 0)
    start(has_above, up_far)
    start(has_below, down_far)
    for _, coming, copies, _, _ in diagonals:
        arrive(coming, copies)
    arrive(has_below, up_near)
    arrive(has_above, down_near)
    set_growth(0)
    set_growth(rows + 1)
    own_row(2, False, True)
    own_row(rows + 1, True, False)

    arrive(has_below, up_far)
    arrive(has_above, down_far)

    @pl.when(has_below)
    def _():
        halo_row(1, 0, 0)

    @pl.when(jnp.logical_not(has_below))
    def _():
        no_halo_row(1, 0)

    @pl.when(has_above)
    def _():
        halo_row(rows + 2, rows - 1, 2)

    @pl.when(jnp.logical_not(has_above))
    def _():
        no_halo_row(rows + 2, 2)

    place = lax.broadcasted_iota(jnp.int32, (rows, cols), 0)

    def beside_rows(x):
        return jnp.where(place == 0, 0.0, pltpu.roll(x, 1, 0)) + jnp.where(
            place == rows - 1, 0.0, pltpu.roll(x, rows - 1, 0)
        )

    term, blend, dterm, dblend = [jnp.sum(accs[q], axis=1) for q in range(4)]
    x_low, q_low, x_high, q_high = [jnp.sum(cross[q], axis=0, keepdims=True) for q in range(4)]
    own_s = term + lanes(blend) + beside_rows(blend)
    own_d = dterm + lanes(dblend) + beside_rows(dblend)
    own_d = own_d + jnp.where(place == 0, q_low, 0.0) + jnp.where(place == rows - 1, q_high, 0.0)
    low_d = dblend[0:1] + x_low + lanes(q_low)
    high_d = dblend[rows - 1 : rows] + x_high + lanes(q_high)
    line = jnp.zeros((1, cols), jnp.float32)
    own_out[0:rows] = own_s
    own_out[rows : 2 * rows] = own_d
    tail = 2 * rows
    halo = [line, blend[0:1], blend[rows - 1 : rows], line, q_low, low_d, high_d, q_high]
    for n, value in enumerate(halo):
        own_out[tail + n : tail + n + 1] = value
    up_out[0:2] = own_s[rows - 2 : rows]
    up_out[2:3] = halo[2]
    up_out[3:4] = line
    up_out[4:6] = own_d[rows - 2 : rows]
    up_out[6:7] = high_d
    up_out[7:8] = q_high
    down_out[0:1] = line
    down_out[1:2] = halo[1]
    down_out[2:4] = own_s[0:2]
    down_out[4:5] = q_low
    down_out[5:6] = low_d
    down_out[6:8] = own_d[0:2]

    def message(src, inbox, sends, receives, n, slot, tt, dd):
        return pltpu.make_async_remote_copy(
            src_ref=src,
            dst_ref=inbox.at[slot],
            send_sem=sends.at[n],
            recv_sem=receives.at[slot],
            device_id=(tt, dd),
            device_id_type=MESH,
        )

    own_messages = [
        message(own_out, own_in, own_send, own_recv, n - 1, d, t, lax.rem(d + n, nd))
        for n in range(1, nd)
    ]
    up_messages = [message(up_out, up_in, up_send, up_recv, n, d, above, n) for n in range(nd)]
    down_messages = [
        message(down_out, down_in, down_send, down_recv, n, d, below, n) for n in range(nd)
    ]
    start(has_above, up_messages)
    start(has_below, down_messages)
    for copy in own_messages:
        copy.start()
    own_in[d] = own_out[...]

    @pl.when(jnp.logical_not(has_below))
    def _():
        for n in range(nd):
            up_in[n] = tile_zero

    @pl.when(jnp.logical_not(has_above))
    def _():
        for n in range(nd):
            down_in[n] = tile_zero

    ext[...] = jnp.zeros_like(ext)
    for n in range(1, nd):
        slot = lax.rem(d + n, nd)
        message(own_out, own_in, own_send, own_recv, n - 1, slot, t, slot).wait_recv()

    @pl.when(has_below)
    def _():
        for n in range(nd):
            message(up_out, up_in, up_send, up_recv, n, n, above, n).wait_recv()

    @pl.when(has_above)
    def _():
        for n in range(nd):
            message(down_out, down_in, down_send, down_recv, n, n, below, n).wait_recv()

    total, low, high = own_in[0], up_in[0], down_in[0]
    for n in range(1, nd):
        total, low, high = total + own_in[n], low + up_in[n], high + down_in[n]
    for q in range(2):
        ext[q, 0:2] = total[tail + 4 * q : tail + 4 * q + 2] + low[4 * q : 4 * q + 2]
        ext[q, 2 : 2 + rows] = total[q * rows : (q + 1) * rows]
        ext[q, 2:4] += low[4 * q + 2 : 4 * q + 4]
        ext[q, rows : rows + 2] += high[4 * q : 4 * q + 2]
        ext[q, rows + 2 : rows + 4] = (
            total[tail + 4 * q + 2 : tail + 4 * q + 4] + high[4 * q + 2 : 4 * q + 4]
        )
    root = math.sqrt(depth * nd)
    high_rows = ext.shape[1]
    bright = jnp.exp(-ext[0] / root)
    change = -bright * ext[1] / root
    mask = maske[rows - 2 : rows - 2 + high_rows].astype(jnp.float32)
    where = lax.broadcasted_iota(jnp.int32, (high_rows, cols), 0)
    valid = jnp.where(has_below, 0, 2)
    valid_end = jnp.where(has_above, rows + 4, rows + 2)
    inside_rows = (where >= valid) & (where < valid_end)
    back = jnp.where(inside_rows, -bright * mask * change, 0.0)
    change_ref[...] = -change[2 : 2 + rows]
    flat = pltpu.roll(back, 1, 0) + pltpu.roll(back, high_rows - 1, 0) + lanes(back) - 4.0 * back
    flat = jnp.where(inside_rows, flat, 0.0)
    g = 0.5 * back + 0.1 * flat
    h = back + 0.1 * flat
    for j in range(rows + 2):
        bb[j] = jnp.broadcast_to(back[j + 1 : j + 2], (8, cols))
        gb[j] = jnp.broadcast_to(g[j + 1 : j + 2], (8, cols))
        hb[j] = jnp.broadcast_to(h[j + 1 : j + 2], (8, cols))

    def carry_row(j, carry):
        b, gg, hh = [tiles(x[j], CH // 8) for x in (bb, gb, hb)]
        for n in range(chunks):
            span = slice(PAD - 8 + n * CH, PAD - 8 + (n + 1) * CH)
            c1[j, span] = gg + c1[j, span] * b
            a1[j, span] = hh + a1[j, span] * b
        return carry

    lax.fori_loop(0, rows + 2, carry_row, 0)

    def no_depth(condition, span):
        @pl.when(jnp.logical_not(condition))
        def _():
            for j in range(rows + 2):
                c1[j, span] = tile_zero
                a1[j, span] = tile_zero

    no_depth(has_left, before)
    no_depth(has_right, after)

    def near(ref, j, k0):
        size = BC + 16
        block = ref[j, k0 - 8 : k0 - 8 + size]
        beside = pltpu.roll(block, 1, 0) + pltpu.roll(block, size - 1, 0)
        center = block[8 : 8 + BC]
        span = slice(k0, k0 + BC)
        return center, beside[8 : 8 + BC] + lanes(center) + ref[j - 1, span] + ref[j + 1, span]

    def out_copies(j):
        return [
            pltpu.make_async_copy(hp.at[j], hp_hbm.at[j], out_sem.at[0, j]),
            pltpu.make_async_copy(hs.at[j], hs_hbm.at[j], out_sem.at[1, j]),
        ]

    def finish(j, carry):
        for n in range(depth // BC):
            k0 = PAD + n * BC
            c, near_c = near(c1, j + 1, k0)
            a, near_a = near(a1, j + 1, k0)
            span = slice(k0, k0 + BC)
            dst = slice(n * BC, (n + 1) * BC)
            hp[j, dst] = 0.5 * a - c * wide[j, span] - 0.1 * near_c
            hs[j, dst] = -0.4 * a - 0.1 * near_a - solw[j, span] * c
        for copy in out_copies(j):
            copy.start()
        return carry

    lax.fori_loop(0, rows, finish, 0)
    for copy in own_messages:
        copy.wait_send()
    sent(has_above, up_messages + up_near + up_far)
    sent(has_below, down_messages + down_near + down_far)
    sent(has_right, to_right)
    sent(has_left, to_left)
    for going, coming, copies, _, _ in diagonals:
        sent(going, copies)
    for j in range(rows):
        for copy in out_copies(j):
            copy.wait()


def local(nt, nd, phase, solute, dphase, dsolute, labels, pixel_mask):
    rows, depth, cols = phase.shape
    f32, i32 = jnp.float32, jnp.int32
    length = depth + 2 * PAD
    dma = pltpu.SemaphoreType.DMA
    any_space = pl.BlockSpec(memory_space=pl.ANY)
    vmem = pl.BlockSpec(memory_space=pltpu.VMEM)
    field = jax.ShapeDtypeStruct((rows, depth, cols), f32)
    negated = pl.pallas_call(
        functools.partial(kernel, nt, nd),
        out_shape=(field, field, jax.ShapeDtypeStruct((rows, cols), f32)),
        in_specs=[any_space] * 6,
        out_specs=(any_space, any_space, vmem),
        scratch_shapes=[
            pltpu.VMEM((rows + 4, length, cols), f32),
            pltpu.VMEM((rows + 4, length, cols), f32),
            pltpu.VMEM((rows, length, cols), f32),
            pltpu.VMEM((rows, length, cols), f32),
            pltpu.VMEM((3 * rows, cols), i32),
            pltpu.VMEM((3 * rows, cols), i32),
            pltpu.VMEM((rows + 2, 8, cols), f32),
            pltpu.VMEM((rows + 2, length, cols), f32),
            pltpu.VMEM((rows + 2, length, cols), f32),
            pltpu.VMEM((rows, length, cols), f32),
            pltpu.VMEM((rows, length, cols), f32),
            pltpu.VMEM((rows, depth, cols), f32),
            pltpu.VMEM((rows, depth, cols), f32),
            pltpu.VMEM((4, rows, 8, cols), f32),
            pltpu.VMEM((4, 8, cols), f32),
            pltpu.VMEM((2 * rows + 8, cols), f32),
            pltpu.VMEM((8, cols), f32),
            pltpu.VMEM((8, cols), f32),
            pltpu.VMEM((nd, 2 * rows + 8, cols), f32),
            pltpu.VMEM((nd, 8, cols), f32),
            pltpu.VMEM((nd, 8, cols), f32),
            pltpu.VMEM((2, rows + 8, cols), f32),
            pltpu.VMEM((rows + 2, 8, cols), f32),
            pltpu.VMEM((rows + 2, 8, cols), f32),
            pltpu.VMEM((rows + 2, 8, cols), f32),
            dma((6,)),
            dma((2, rows)),
            dma((28,)),
            dma((28,)),
            dma((nd - 1,)),
            dma((nd,)),
            dma((nd,)),
            dma((nd,)),
            dma((nd,)),
            dma((nd,)),
        ],
        compiler_params=pltpu.CompilerParams(
            collective_id=0, has_side_effects=True, vmem_limit_bytes=63 * 1024 * 1024
        ),
    )(phase, solute, dphase, dsolute, labels, pixel_mask)
    return tuple(-value for value in negated)


def solution(mesh):
    field, plane = P("tile", "depth", None), P("tile", None)
    return jax.shard_map(
        functools.partial(local, mesh.shape["tile"], mesh.shape["depth"]),
        mesh=mesh,
        in_specs=(field, field, field, field, plane, plane),
        out_specs=(field, field, plane),
        check_vma=False,
    )
```

```python
import functools
import math

import jax
import jax.numpy as jnp
from jax import lax
from jax.experimental import pallas as pl
from jax.experimental.pallas import tpu as pltpu
from jax.sharding import PartitionSpec as P

MESH = pl.DeviceIdType.MESH
PAD = 16
CH = 48
BC = 32


def growth(labels):
    return jnp.where(
        labels == 0, 0.6, jnp.where(labels == 1, 1.0, jnp.where(labels == 2, 1.7, 0.8))
    ).astype(jnp.float32)


def slopes(p, s, grow):
    shell = 1.0 - p * p
    return grow * (1.0 - 3.0 * p * p) + 4.0 * p * shell * s, -shell * shell


def tiles(block, count):
    return jnp.concatenate([block] * count, axis=0)


def fold(value):
    total = value[0:8]
    for k in range(8, value.shape[0], 8):
        total = total + value[k : k + 8]
    return total


def lanes(value):
    cols = value.shape[1]
    lane = lax.broadcasted_iota(jnp.int32, value.shape, 1)
    left = jnp.where(lane == 0, 0.0, pltpu.roll(value, 1, 1))
    right = jnp.where(lane == cols - 1, 0.0, pltpu.roll(value, cols - 1, 1))
    return left + right


def kernel(
    nt, nd,
    p_hbm, s_hbm, dp_hbm, ds_hbm, lab_hbm, mask_hbm,
    hp_hbm, hs_hbm, change_ref,
    pe, se, dpe, dse, labe, maske, growb,
    c1, a1, wide, solw, hp, hs,
    accs, cross, own_out, up_out, down_out, own_in, up_in, down_in,
    ext, bb, gb, hb,
    local_sem, out_sem, send_sem, recv_sem, own_send, own_recv, up_send, up_recv, down_send, down_recv,
):
    rows, depth, cols = p_hbm.shape
    t = lax.axis_index("tile")
    d = lax.axis_index("depth")
    has_above, has_below = t < nt - 1, t > 0
    has_right, has_left = d < nd - 1, d > 0
    above, below = lax.rem(t + 1, nt), lax.rem(t + nt - 1, nt)
    right, left = lax.rem(d + 1, nd), lax.rem(d + nd - 1, nd)
    end = PAD + depth
    core = slice(PAD, end)
    core_rows = slice(2, 2 + rows)

    local = [
        pltpu.make_async_copy(src, dst, local_sem.at[n])
        for n, (src, dst) in enumerate(
            [
                (p_hbm, pe.at[core_rows, core]),
                (s_hbm, se.at[core_rows, core]),
                (dp_hbm, dpe.at[:, core]),
                (ds_hbm, dse.at[:, core]),
                (lab_hbm, labe.at[rows : 2 * rows]),
                (mask_hbm, maske.at[rows : 2 * rows]),
            ]
        )
    ]
    for copy in local:
        copy.start()

    barrier = pltpu.get_barrier_semaphore()

    def greet(tt, dd):
        pl.semaphore_signal(barrier, inc=1, device_id=(tt, dd), device_id_type=MESH)

    for n in range(1, nd):
        greet(t, lax.rem(d + n, nd))

    @pl.when(has_above)
    def _():
        for n in range(nd):
            greet(above, n)

    @pl.when(has_below)
    def _():
        for n in range(nd):
            greet(below, n)

    beside_count = jnp.where(has_above, 1, 0) + jnp.where(has_below, 1, 0)
    pl.semaphore_wait(barrier, nd - 1 + nd * beside_count)

    number = [0]

    def remote(src, dst, tt, dd):
        n = number[0]
        number[0] = n + 1
        return pltpu.make_async_remote_copy(
            src_ref=src,
            dst_ref=dst,
            send_sem=send_sem.at[n],
            recv_sem=recv_sem.at[n],
            device_id=(tt, dd),
            device_id_type=MESH,
        )

    top, bottom = 2 + rows, 1
    first, last = slice(0, 8), slice(depth - 8, depth)
    after, before = slice(end, end + 8), slice(PAD - 8, PAD)
    pairs = [(p_hbm, pe), (s_hbm, se)]
    to_right = [remote(a.at[:, last], b.at[core_rows, before], t, right) for a, b in pairs]
    to_left = [remote(a.at[:, first], b.at[core_rows, after], t, left) for a, b in pairs]
    for a, b in [(dp_hbm, dpe), (ds_hbm, dse)]:
        to_right.append(remote(a.at[:, last], b.at[:, before], t, right))
        to_left.append(remote(a.at[:, first], b.at[:, after], t, left))
    diagonals = []
    for tt, going_t, coming_t, src_row, dst_row in [
        (above, has_above, has_below, rows - 1, bottom),
        (below, has_below, has_above, 0, top),
    ]:
        for dd, going_d, coming_d, src_k, dst_k in [
            (right, has_right, has_left, last, before),
            (left, has_left, has_right, first, after),
        ]:
            copies = [
                remote(a.at[pl.ds(src_row, 1), src_k], b.at[pl.ds(dst_row, 1), dst_k], tt, dd)
                for a, b in pairs
            ]
            diagonals.append((going_t & going_d, coming_t & coming_d, copies, dst_row, dst_k))
    up_near = [remote(lab_hbm, labe.at[0:rows], above, d), remote(mask_hbm, maske.at[0:rows], above, d)]
    down_near = [
        remote(lab_hbm, labe.at[2 * rows : 3 * rows], below, d),
        remote(mask_hbm, maske.at[2 * rows : 3 * rows], below, d),
    ]
    for a, b in pairs:
        up_near.append(remote(a.at[pl.ds(rows - 1, 1)], b.at[pl.ds(1, 1), core], above, d))
        down_near.append(remote(a.at[pl.ds(0, 1)], b.at[pl.ds(top, 1), core], below, d))
    up_far = [remote(a.at[pl.ds(rows - 2, 1)], b.at[pl.ds(0, 1), core], above, d) for a, b in pairs]
    down_far = [remote(a.at[pl.ds(1, 1)], b.at[pl.ds(top + 1, 1), core], below, d) for a, b in pairs]

    def start(condition, copies):
        @pl.when(condition)
        def _():
            for copy in copies:
                copy.start()

    def arrive(condition, copies):
        @pl.when(condition)
        def _():
            for copy in copies:
                copy.wait_recv()

    def sent(condition, copies):
        @pl.when(condition)
        def _():
            for copy in copies:
                copy.wait_send()

    start(has_above, up_near)
    start(has_below, down_near)
    start(has_right, to_right)
    start(has_left, to_left)
    for going, coming, copies, _, _ in diagonals:
        start(going, copies)

    row_zero = jnp.zeros((depth, cols), jnp.float32)
    tile_zero = jnp.zeros((8, cols), jnp.float32)
    label_zero = jnp.zeros((rows, cols), jnp.int32)

    def no_row(condition, near, far, label_at):
        @pl.when(jnp.logical_not(condition))
        def _():
            for b in (pe, se):
                b[near, core] = row_zero
                b[far, core] = row_zero
            labe[label_at : label_at + rows] = label_zero
            maske[label_at : label_at + rows] = label_zero

    no_row(has_below, 1, 0, 0)
    no_row(has_above, top, top + 1, 2 * rows)

    def no_side(condition, span):
        @pl.when(jnp.logical_not(condition))
        def _():
            for r in range(rows):
                pe[2 + r, span] = tile_zero
                se[2 + r, span] = tile_zero
                dpe[r, span] = tile_zero
                dse[r, span] = tile_zero

    no_side(has_left, before)
    no_side(has_right, after)
    for _, coming, _, dst_row, dst_k in diagonals:

        @pl.when(jnp.logical_not(coming))
        def _():
            pe[dst_row, dst_k] = tile_zero
            se[dst_row, dst_k] = tile_zero

    for copy in local:
        copy.wait()

    def set_growth(j):
        row = labe[rows - 1 + j : rows + j]
        growb[j] = jnp.broadcast_to(growth(row), (8, cols))

    for j in range(1, rows + 1):
        set_growth(j)

    sub = lax.broadcasted_iota(jnp.int32, (CH, cols), 0)
    low_end = jnp.where(d == 0, PAD, -1)
    high_end = jnp.where(d == nd - 1, end - 1, -1)

    def spread(ref, r, k0):
        block = ref[r, pl.ds(pl.multiple_of(k0 - 8, 8), CH + 16), :]
        size = CH + 16
        beside = pltpu.roll(block, 1, 0) + pltpu.roll(block, size - 1, 0)
        center = block[8 : 8 + CH]
        return center, beside[8 : 8 + CH] + lanes(center) - 6.0 * center

    def at(ref, r, k0):
        return ref[r, pl.ds(pl.multiple_of(k0, 8), CH), :]

    def base_next(i, k0, grow):
        p, lap_p = spread(pe, i, k0)
        s, lap_s = spread(se, i, k0)
        lap_p = lap_p + at(pe, i - 1, k0) + at(pe, i + 1, k0)
        lap_s = lap_s + at(se, i - 1, k0) + at(se, i + 1, k0)
        shell = 1.0 - p * p
        p_next = p + 0.1 * (lap_p + grow * (p - p * p * p) - shell * shell * s)
        s_next = s + 0.1 * lap_s + 0.5 * (p_next - p)
        return p, s, p_next, s_next

    def save_slopes(i, k0, slope_p, slope_s, at_end):
        span = pl.ds(pl.multiple_of(k0, 8), CH)
        c1[i - 1, span, :] = 0.05 * slope_p + 0.025 * slope_s - 0.1 * at_end
        a1[i - 1, span, :] = 0.05 * slope_s - 0.1 * at_end

    def ends_of(k0):
        k = sub + k0
        at_end = jnp.where((k == low_end) | (k == high_end), 1.0, 0.0)
        inside = (k >= PAD) & (k < end)
        return at_end, inside

    chunks = (depth + 16) // CH

    def own_row(i, has_lower, has_upper):
        j = i - 2
        grow = tiles(growb[i - 1], CH // 8)

        def one(n, carry):
            k0 = PAD - 8 + n * CH
            at_end, inside = ends_of(k0)
            p, s, p1, s1 = base_next(i, k0, grow)
            slope_p, slope_s = slopes(p, s, grow)
            span = pl.ds(pl.multiple_of(k0, 8), CH)
            wide[j, span, :] = 0.4 + 0.1 * slope_p
            solw[j, span, :] = 0.1 * slope_s
            next_p, next_s = slopes(p1, s1, grow)
            save_slopes(i, k0, next_p, next_s, at_end)
            dp, lap_dp = spread(dpe, j, k0)
            ds, lap_ds = spread(dse, j, k0)
            if has_lower:
                lap_dp = lap_dp + at(dpe, j - 1, k0)
                lap_ds = lap_ds + at(dse, j - 1, k0)
            if has_upper:
                lap_dp = lap_dp + at(dpe, j + 1, k0)
                lap_ds = lap_ds + at(dse, j + 1, k0)
            dp1 = dp + 0.1 * (lap_dp + slope_p * dp + slope_s * ds)
            ds1 = ds + 0.1 * lap_ds + 0.5 * (dp1 - dp)
            weight = 4.0 + at_end
            blend = 0.1 * s1 + 0.05 * p1
            dblend = 0.1 * ds1 + 0.05 * dp1
            term = s1 + 0.05 * (grow * (p1 - p1 * p1 * p1) + next_s * s1) - weight * blend
            dterm = ds1 + 0.05 * (next_p * dp1 + next_s * ds1) - weight * dblend
            parts = (term, blend, dterm, dblend)
            return tuple(c + fold(jnp.where(inside, v, 0.0)) for c, v in zip(carry, parts))

        zero = jnp.zeros((8, cols), jnp.float32)
        sums = lax.fori_loop(0, chunks, one, (zero, zero, zero, zero))
        for q in range(4):
            accs[q, j] = sums[q]

    def halo_row(i, j, slot):
        grow = tiles(growb[i - 1], CH // 8)

        def one(n, carry):
            k0 = PAD - 8 + n * CH
            at_end, inside = ends_of(k0)
            _, _, p1, s1 = base_next(i, k0, grow)
            next_p, next_s = slopes(p1, s1, grow)
            save_slopes(i, k0, next_p, next_s, at_end)
            dp, ds = at(dpe, j, k0), at(dse, j, k0)
            add_p = 0.1 * dp
            add_s = 0.1 * ds + 0.05 * dp
            dblend = 0.1 * add_s + 0.05 * add_p
            dterm = add_s + 0.05 * (next_p * add_p + next_s * add_s) - (4.0 + at_end) * dblend
            return tuple(
                c + fold(jnp.where(inside, v, 0.0)) for c, v in zip(carry, (dterm, dblend))
            )

        zero = jnp.zeros((8, cols), jnp.float32)
        sums = lax.fori_loop(0, chunks, one, (zero, zero))
        cross[slot] = sums[0]
        cross[slot + 1] = sums[1]

    def no_halo_row(i, slot):
        c1[i - 1] = jnp.zeros((end + PAD, cols), jnp.float32)
        a1[i - 1] = jnp.zeros((end + PAD, cols), jnp.float32)
        cross[slot] = tile_zero
        cross[slot + 1] = tile_zero

    arrive(has_left, to_right)
    arrive(has_right, to_left)

    def middle(i, carry):
        own_row(i, True, True)
        return carry

    lax.fori_loop(3, rows + 1, middle, 0)
    start(has_above, up_far)
    start(has_below, down_far)
    for _, coming, copies, _, _ in diagonals:
        arrive(coming, copies)
    arrive(has_below, up_near)
    set_growth(0)
    own_row(2, False, True)
    arrive(has_above, down_near)
    set_growth(rows + 1)
    own_row(rows + 1, True, False)

    arrive(has_below, up_far)

    @pl.when(has_below)
    def _():
        halo_row(1, 0, 0)

    @pl.when(jnp.logical_not(has_below))
    def _():
        no_halo_row(1, 0)

    arrive(has_above, down_far)

    @pl.when(has_above)
    def _():
        halo_row(rows + 2, rows - 1, 2)

    @pl.when(jnp.logical_not(has_above))
    def _():
        no_halo_row(rows + 2, 2)

    place = lax.broadcasted_iota(jnp.int32, (rows, cols), 0)

    def beside_rows(x):
        return jnp.where(place == 0, 0.0, pltpu.roll(x, 1, 0)) + jnp.where(
            place == rows - 1, 0.0, pltpu.roll(x, rows - 1, 0)
        )

    term, blend, dterm, dblend = [jnp.sum(accs[q], axis=1) for q in range(4)]
    x_low, q_low, x_high, q_high = [jnp.sum(cross[q], axis=0, keepdims=True) for q in range(4)]
    own_s = term + lanes(blend) + beside_rows(blend)
    own_d = dterm + lanes(dblend) + beside_rows(dblend)
    own_d = own_d + jnp.where(place == 0, q_low, 0.0) + jnp.where(place == rows - 1, q_high, 0.0)
    low_d = dblend[0:1] + x_low + lanes(q_low)
    high_d = dblend[rows - 1 : rows] + x_high + lanes(q_high)
    line = jnp.zeros((1, cols), jnp.float32)
    own_out[0:rows] = own_s
    own_out[rows : 2 * rows] = own_d
    tail = 2 * rows
    halo = [line, blend[0:1], blend[rows - 1 : rows], line, q_low, low_d, high_d, q_high]
    for n, value in enumerate(halo):
        own_out[tail + n : tail + n + 1] = value
    up_out[0:2] = own_s[rows - 2 : rows]
    up_out[2:3] = halo[2]
    up_out[3:4] = line
    up_out[4:6] = own_d[rows - 2 : rows]
    up_out[6:7] = high_d
    up_out[7:8] = q_high
    down_out[0:1] = line
    down_out[1:2] = halo[1]
    down_out[2:4] = own_s[0:2]
    down_out[4:5] = q_low
    down_out[5:6] = low_d
    down_out[6:8] = own_d[0:2]

    def message(src, inbox, sends, receives, n, slot, tt, dd):
        return pltpu.make_async_remote_copy(
            src_ref=src,
            dst_ref=inbox.at[slot],
            send_sem=sends.at[n],
            recv_sem=receives.at[slot],
            device_id=(tt, dd),
            device_id_type=MESH,
        )

    own_messages = [
        message(own_out, own_in, own_send, own_recv, n - 1, d, t, lax.rem(d + n, nd))
        for n in range(1, nd)
    ]
    up_messages = [message(up_out, up_in, up_send, up_recv, n, d, above, n) for n in range(nd)]
    down_messages = [
        message(down_out, down_in, down_send, down_recv, n, d, below, n) for n in range(nd)
    ]
    start(has_above, up_messages)
    start(has_below, down_messages)
    for copy in own_messages:
        copy.start()
    own_in[d] = own_out[...]

    @pl.when(jnp.logical_not(has_below))
    def _():
        for n in range(nd):
            up_in[n] = tile_zero

    @pl.when(jnp.logical_not(has_above))
    def _():
        for n in range(nd):
            down_in[n] = tile_zero

    ext[...] = jnp.zeros_like(ext)
    for n in range(1, nd):
        slot = lax.rem(d + n, nd)
        message(own_out, own_in, own_send, own_recv, n - 1, slot, t, slot).wait_recv()

    @pl.when(has_below)
    def _():
        for n in range(nd):
            message(up_out, up_in, up_send, up_recv, n, n, above, n).wait_recv()

    @pl.when(has_above)
    def _():
        for n in range(nd):
            message(down_out, down_in, down_send, down_recv, n, n, below, n).wait_recv()

    total, low, high = own_in[0], up_in[0], down_in[0]
    for n in range(1, nd):
        total, low, high = total + own_in[n], low + up_in[n], high + down_in[n]
    for q in range(2):
        ext[q, 0:2] = total[tail + 4 * q : tail + 4 * q + 2] + low[4 * q : 4 * q + 2]
        ext[q, 2 : 2 + rows] = total[q * rows : (q + 1) * rows]
        ext[q, 2:4] += low[4 * q + 2 : 4 * q + 4]
        ext[q, rows : rows + 2] += high[4 * q : 4 * q + 2]
        ext[q, rows + 2 : rows + 4] = (
            total[tail + 4 * q + 2 : tail + 4 * q + 4] + high[4 * q + 2 : 4 * q + 4]
        )
    root = math.sqrt(depth * nd)
    high_rows = ext.shape[1]
    bright = jnp.exp(-ext[0] / root)
    change = -bright * ext[1] / root
    mask = maske[rows - 2 : rows - 2 + high_rows].astype(jnp.float32)
    where = lax.broadcasted_iota(jnp.int32, (high_rows, cols), 0)
    valid = jnp.where(has_below, 0, 2)
    valid_end = jnp.where(has_above, rows + 4, rows + 2)
    inside_rows = (where >= valid) & (where < valid_end)
    back = jnp.where(inside_rows, -bright * mask * change, 0.0)
    change_ref[...] = -change[2 : 2 + rows]
    flat = pltpu.roll(back, 1, 0) + pltpu.roll(back, high_rows - 1, 0) + lanes(back) - 4.0 * back
    flat = jnp.where(inside_rows, flat, 0.0)
    g = 0.5 * back + 0.1 * flat
    h = back + 0.1 * flat
    for j in range(rows + 2):
        bb[j] = jnp.broadcast_to(back[j + 1 : j + 2], (8, cols))
        gb[j] = jnp.broadcast_to(g[j + 1 : j + 2], (8, cols))
        hb[j] = jnp.broadcast_to(h[j + 1 : j + 2], (8, cols))

    def carry_row(j, carry):
        b, gg, hh = [tiles(x[j], CH // 8) for x in (bb, gb, hb)]
        for n in range(chunks):
            span = slice(PAD - 8 + n * CH, PAD - 8 + (n + 1) * CH)
            c1[j, span] = gg + c1[j, span] * b
            a1[j, span] = hh + a1[j, span] * b
        return carry

    lax.fori_loop(0, rows + 2, carry_row, 0)

    def no_depth(condition, span):
        @pl.when(jnp.logical_not(condition))
        def _():
            for j in range(rows + 2):
                c1[j, span] = tile_zero
                a1[j, span] = tile_zero

    no_depth(has_left, before)
    no_depth(has_right, after)

    def near(ref, j, k0):
        size = BC + 16
        block = ref[j, k0 - 8 : k0 - 8 + size]
        beside = pltpu.roll(block, 1, 0) + pltpu.roll(block, size - 1, 0)
        center = block[8 : 8 + BC]
        span = slice(k0, k0 + BC)
        return center, beside[8 : 8 + BC] + lanes(center) + ref[j - 1, span] + ref[j + 1, span]

    def out_copies(j):
        return [
            pltpu.make_async_copy(hp.at[j], hp_hbm.at[j], out_sem.at[0, j]),
            pltpu.make_async_copy(hs.at[j], hs_hbm.at[j], out_sem.at[1, j]),
        ]

    def finish(j, carry):
        for n in range(depth // BC):
            k0 = PAD + n * BC
            c, near_c = near(c1, j + 1, k0)
            a, near_a = near(a1, j + 1, k0)
            span = slice(k0, k0 + BC)
            dst = slice(n * BC, (n + 1) * BC)
            hp[j, dst] = 0.5 * a - c * wide[j, span] - 0.1 * near_c
            hs[j, dst] = -0.4 * a - 0.1 * near_a - solw[j, span] * c
        for copy in out_copies(j):
            copy.start()
        return carry

    lax.fori_loop(0, rows, finish, 0)
    for copy in own_messages:
        copy.wait_send()
    sent(has_above, up_messages + up_near + up_far)
    sent(has_below, down_messages + down_near + down_far)
    sent(has_right, to_right)
    sent(has_left, to_left)
    for going, coming, copies, _, _ in diagonals:
        sent(going, copies)
    for j in range(rows):
        for copy in out_copies(j):
            copy.wait()


def local(nt, nd, phase, solute, dphase, dsolute, labels, pixel_mask):
    rows, depth, cols = phase.shape
    f32, i32 = jnp.float32, jnp.int32
    length = depth + 2 * PAD
    dma = pltpu.SemaphoreType.DMA
    any_space = pl.BlockSpec(memory_space=pl.ANY)
    vmem = pl.BlockSpec(memory_space=pltpu.VMEM)
    field = jax.ShapeDtypeStruct((rows, depth, cols), f32)
    negated = pl.pallas_call(
        functools.partial(kernel, nt, nd),
        out_shape=(field, field, jax.ShapeDtypeStruct((rows, cols), f32)),
        in_specs=[any_space] * 6,
        out_specs=(any_space, any_space, vmem),
        scratch_shapes=[
            pltpu.VMEM((rows + 4, length, cols), f32),
            pltpu.VMEM((rows + 4, length, cols), f32),
            pltpu.VMEM((rows, length, cols), f32),
            pltpu.VMEM((rows, length, cols), f32),
            pltpu.VMEM((3 * rows, cols), i32),
            pltpu.VMEM((3 * rows, cols), i32),
            pltpu.VMEM((rows + 2, 8, cols), f32),
            pltpu.VMEM((rows + 2, length, cols), f32),
            pltpu.VMEM((rows + 2, length, cols), f32),
            pltpu.VMEM((rows, length, cols), f32),
            pltpu.VMEM((rows, length, cols), f32),
            pltpu.VMEM((rows, depth, cols), f32),
            pltpu.VMEM((rows, depth, cols), f32),
            pltpu.VMEM((4, rows, 8, cols), f32),
            pltpu.VMEM((4, 8, cols), f32),
            pltpu.VMEM((2 * rows + 8, cols), f32),
            pltpu.VMEM((8, cols), f32),
            pltpu.VMEM((8, cols), f32),
            pltpu.VMEM((nd, 2 * rows + 8, cols), f32),
            pltpu.VMEM((nd, 8, cols), f32),
            pltpu.VMEM((nd, 8, cols), f32),
            pltpu.VMEM((2, rows + 8, cols), f32),
            pltpu.VMEM((rows + 2, 8, cols), f32),
            pltpu.VMEM((rows + 2, 8, cols), f32),
            pltpu.VMEM((rows + 2, 8, cols), f32),
            dma((6,)),
            dma((2, rows)),
            dma((28,)),
            dma((28,)),
            dma((nd - 1,)),
            dma((nd,)),
            dma((nd,)),
            dma((nd,)),
            dma((nd,)),
            dma((nd,)),
        ],
        compiler_params=pltpu.CompilerParams(
            collective_id=0, has_side_effects=True, vmem_limit_bytes=63 * 1024 * 1024
        ),
    )(phase, solute, dphase, dsolute, labels, pixel_mask)
    return tuple(-value for value in negated)


def solution(mesh):
    field, plane = P("tile", "depth", None), P("tile", None)
    return jax.shard_map(
        functools.partial(local, mesh.shape["tile"], mesh.shape["depth"]),
        mesh=mesh,
        in_specs=(field, field, field, field, plane, plane),
        out_specs=(field, field, plane),
        check_vma=False,
    )
```
